32 devices in a mesh: ctx: 4 (over y, x), tp: 8 (over z, core).
Axes of the slice: x: 2, y: 2, z: 4, core: 2. Of those that a mesh axis runs over, the one named last changes fastest.
Arguments:
- token_ids: int32 [1536], P('ctx'), may hold values from 65 to 84, as said below
- embed_table: bfloat16 [512, 4096], replicated, may hold values from -6 to 6
- norm_gain: float32 [4096], replicated, may hold values from 0.5 to 1.5
- input_weight: bfloat16 [4096, 3, 4096], P(None, None, 'tp'), may hold values from -0.09375 to 0.09375
- short_weight: float32 [3, 3, 4096], P(None, None, 'tp'), may hold values from -3 to 3
- filters: float32 [256, 1536], P('tp', 'ctx'), may hold values from -1.1 to 1.1
- skip_gain: float32 [4096], P('tp'), may hold values from 0.1 to 1.9
- output_weight: bfloat16 [4096, 4096], P(None, 'tp'), may hold values from -0.09375 to 0.09375
- output_grad: bfloat16 [1536, 4096], P('ctx'), may hold values from -6 to 6
Outputs:
- block_output: bfloat16 [1536, 4096], P('ctx')
- output_weight_grad: float32 [4096, 4096], P('ctx', 'tp')
- projection_grad: bfloat16 [1536, 3, 4096], P('ctx', None, 'tp')
- normed_grad: float32 [1536, 4096], P(('ctx', 'tp'))
The draws below stay inside these ranges and needn't reach their ends.
Inputs may be any that keep to these rules, and one draw needn't show every extreme that they name: `token_ids`: each id is the byte code of A, C, G, T or N.
All inputs are finite; a program needn't handle non-finite values.
Results may differ from the reference program's by a relative error of at most 0.0065.
Values may be sent and summed in bfloat16 or wider, within the bound.
No kernel may reach another device: no remote copies, remote signals or barrier semaphores. Data moves between devices by JAX's collectives and lax.ppermute only.
A program may use at most 256 MiB of HBM per device.

```python
import jax
import jax.numpy as jnp
from jax import lax

D = 4096
VOCAB = 512
GROUPS = 256
SHORT = 3
TOKENS = 1536


def draw_token_ids(key, part):
    nucleotide_codes = jnp.array([65, 67, 71, 84, 78], dtype=jnp.int32)
    picks = jax.random.randint(key, (TOKENS,), 0, 5)
    picks = picks.at[0].set(0).at[1].set(3)
    return nucleotide_codes[picks]


def draw_filters(key, part):
    rate_key, noise_key = jax.random.split(jax.random.fold_in(key, 17), 2)
    positions = jnp.arange(TOKENS, dtype=jnp.float32)[None, :]
    scales = jnp.exp(jax.random.uniform(rate_key, (GROUPS, 1), minval=jnp.log(30.0), maxval=jnp.log(16.0 * TOKENS)))
    noise = jnp.clip(jax.random.normal(noise_key, (GROUPS, TOKENS)), -4.0, 4.0)
    amplitude = jnp.sqrt(2.0 / scales + 1.0 / TOKENS)
    return (amplitude * noise * jnp.exp(-positions / scales)).astype(jnp.float32)


def levels(stream_key, shape, pieces, low, largest):
    loudness = 1.0
    for dim, shards_of in pieces:
        draws = jax.random.uniform(jax.random.fold_in(jax.random.fold_in(stream_key, 6), dim), (shards_of,), jnp.float32, low / len(pieces), largest / len(pieces))
        loudness = loudness * jnp.repeat(jnp.exp(draws), shape[dim] // shards_of).reshape((-1,) + (1,) * (len(shape) - 1 - dim))
    return loudness


def scatter_about(rng, dims, deviation, most, shards=(), kind=jnp.bfloat16):
    loudness = levels(rng, dims, shards, -0.22, 0.18) if shards else 1.0
    drawn = jax.random.normal(rng, dims, jnp.float32) * deviation * loudness
    return jnp.minimum(jnp.maximum(drawn, -most), most).astype(kind)


def setup_inputs(seed: int = 0) -> dict:
    splits = jax.random.split(jax.random.key(seed), 10)
    token_ids = draw_token_ids(jax.random.fold_in(splits[9], 71), 0)
    embed_table = scatter_about(splits[1], (VOCAB, D), 1.0, 6.0)
    norm_gain = jnp.clip(1.0 + 0.1 * jax.random.normal(splits[2], (D,), jnp.float32), 0.5, 1.5)
    input_weight = scatter_about(splits[3], (D, 3, D), D ** -0.5, 0.09375, ((2, 8),))
    short_weight = scatter_about(splits[4], (SHORT, 3, D), 0.6, 3.0, ((2, 8),), jnp.float32)
    filters = draw_filters(jax.random.fold_in(splits[9], 71), 0)
    skip_gain = jnp.clip(1.0 + 0.18 * jax.random.normal(splits[6], (D,), jnp.float32), 0.1, 1.9)
    output_weight = scatter_about(splits[7], (D, D), D ** -0.5, 0.09375, ((1, 8),))
    output_grad = scatter_about(splits[8], (TOKENS, D), 1.0, 6.0, ((0, 4),))
    return {"token_ids": token_ids, "embed_table": embed_table, "norm_gain": norm_gain, "input_weight": input_weight, "short_weight": short_weight, "filters": filters, "skip_gain": skip_gain, "output_weight": output_weight, "output_grad": output_grad}


def causal_apply(signal, channel_taps, adjoint):
    length = signal.shape[0]
    signal_spec = jnp.fft.rfft(signal, n=2 * length, axis=0)
    filter_spec = jnp.fft.rfft(channel_taps, n=2 * length, axis=0)
    if adjoint:
        filter_spec = jnp.conj(filter_spec)
    return jnp.fft.irfft(signal_spec * filter_spec, n=2 * length, axis=0)[:length].astype(jnp.float32)

def reference(token_ids, embed_table, norm_gain, input_weight, short_weight, filters, skip_gain, output_weight, output_grad):
    tokens = embed_table[token_ids]
    token_values = tokens.astype(jnp.float32)
    inverse_rms = lax.rsqrt(lax.optimization_barrier(jnp.mean(token_values * token_values, axis=-1, keepdims=True)) + 1e-06)
    normed = (token_values * inverse_rms * norm_gain).astype(jnp.bfloat16)
    projected = jnp.einsum('td,djc->tjc', normed.astype(jnp.float32), input_weight.astype(jnp.float32))
    short_taps = short_weight.shape[0]
    length = projected.shape[0]
    padded = jnp.pad(projected, ((short_taps - 1, 0), (0, 0), (0, 0)))
    features = sum((short_weight[tap_index] * padded[short_taps - 1 - tap_index:short_taps - 1 - tap_index + length] for tap_index in range(short_taps)))
    query_part = features[:, 0]
    key_part = features[:, 1]
    value_part = features[:, 2]
    mixture = key_part * value_part
    group_width = mixture.shape[1] // filters.shape[0]
    channel_taps = jnp.repeat(filters.T, group_width, axis=1)
    mixed_out = skip_gain * mixture + causal_apply(mixture, channel_taps, False)
    hidden = (query_part * mixed_out).astype(jnp.bfloat16)
    block_output = (token_values + jnp.dot(hidden, output_weight.T, preferred_element_type=jnp.float32)).astype(jnp.bfloat16)
    hidden_grad = jnp.dot(output_grad, output_weight, preferred_element_type=jnp.float32)
    output_weight_grad = jnp.dot(output_grad.T, hidden, preferred_element_type=jnp.float32)
    mixed_grad = hidden_grad * query_part
    mixture_grad = skip_gain * mixed_grad + causal_apply(mixed_grad, channel_taps, True)
    feature_grad = jnp.stack([hidden_grad * mixed_out, mixture_grad * value_part, mixture_grad * key_part], axis=1)
    padded_grad = jnp.pad(feature_grad, ((0, short_taps - 1), (0, 0), (0, 0)))
    projection_grad = sum((short_weight[tap_index] * padded_grad[tap_index:tap_index + length] for tap_index in range(short_taps))).astype(jnp.bfloat16)
    normed_grad = jnp.einsum('tjc,djc->td', projection_grad.astype(jnp.float32), input_weight.astype(jnp.float32))
    return (block_output, output_weight_grad, projection_grad, normed_grad)
```

```python
import functools

import jax
import jax.numpy as jnp
from jax import lax
from jax.experimental import pallas as pl
from jax.experimental.pallas import tpu as pltpu
from jax.sharding import PartitionSpec as P

LANES = 128
FIRST_ID = 64
IDS = 24
VMEM_BYTES = 60 * 1024 * 1024
f32 = jnp.float32
bf16 = jnp.bfloat16


def one_hot(ids, taps):
    length = ids.shape[1]
    lane = lax.broadcasted_iota(jnp.int32, (1, length), 1)
    code = lax.broadcasted_iota(jnp.int32, (IDS, length), 0) + FIRST_ID
    rows = []
    for tap in range(taps):
        moved = ids if tap == 0 else jnp.where(lane < tap, 0, pltpu.roll(ids, tap, axis=1))
        rows.append(jnp.where(code == moved, 1.0, 0.0))
    return jnp.concatenate(rows, axis=0)


def tap_weights(taps_ref, table_ref, part):
    table = table_ref[part]
    value = jnp.concatenate([taps_ref[i, part][None, :] * table for i in range(taps_ref.shape[0])], axis=0)
    high = value.astype(bf16).astype(f32)
    return jnp.concatenate([high, value - high], axis=0).astype(bf16)


def expand(weights, hot):
    return lax.dot_general(weights, hot, (((0,), (0,)), ((), ())), preferred_element_type=f32)


def toeplitz_tiles(row, blocks):
    sub = lax.broadcasted_iota(jnp.int32, (LANES, LANES), 0)
    lane = lax.broadcasted_iota(jnp.int32, (LANES, LANES), 1)
    keep = lane >= sub
    before = jnp.zeros((LANES, LANES), f32)
    tiles = []
    for q in range(blocks):
        part = jnp.broadcast_to(row[:, LANES * q : LANES * (q + 1)], (LANES, LANES))
        turned = pltpu.roll(part, 0, 1, stride=1, stride_axis=0)
        tiles.append(jnp.where(keep, turned, before).astype(bf16))
        before = turned
    return tiles


def lanes_at(block, count):
    return pl.ds(pl.multiple_of(block * LANES, LANES), count * LANES)


def gather_slots(me, slots, store):
    for step, slot in enumerate(slots):
        store(jnp.bitwise_xor(me, step), slot)


def forward_kernel(shards, me_ref, *refs):
    ids_slots, filter_slots = refs[:shards], refs[shards : 2 * shards]
    table_ref, taps_ref, columns_ref, hidden_ref, mixed_ref = refs[2 * shards : 2 * shards + 5]
    ids_all, hot, filters, signal, exact, long_part = refs[2 * shards + 5 :]
    me = me_ref[0]
    groups, local_rows = filter_slots[0].shape
    channels = table_ref.shape[2]
    width = channels // groups
    local_blocks = local_rows // LANES
    blocks = shards * local_blocks
    length = blocks * LANES
    window = local_blocks + 1

    for step in range(shards):
        place = lanes_at(jnp.bitwise_xor(me, step) * local_blocks, local_blocks)
        ids_all[:, place] = ids_slots[step][...]
        filters[:, place] = filter_slots[step][...]
    marks = one_hot(ids_all[...], taps_ref.shape[0])
    hot[:, :length] = jnp.concatenate([marks, marks], axis=0).astype(bf16)
    hot[:, length:] = jnp.zeros((hot.shape[0], LANES), bf16)

    signal[:, :length] = jnp.zeros((channels, length), bf16)
    signal[:, 2 * length :] = jnp.zeros((channels, LANES), bf16)
    exact[:, length:] = jnp.zeros((channels, LANES), f32)
    key_weights = tap_weights(taps_ref, table_ref, 1)
    value_weights = tap_weights(taps_ref, table_ref, 2)
    for start in range(0, channels, LANES):
        rows = slice(start, start + LANES)
        mixture = expand(key_weights[:, rows], hot[:, :length]) * expand(value_weights[:, rows], hot[:, :length])
        exact[rows, :length] = mixture
        signal[rows, length : 2 * length] = mixture.astype(bf16)

    first = me * local_blocks

    def one_group(group, carry):
        tiles = toeplitz_tiles(filters[pl.ds(group, 1), :], blocks)
        matrix = jnp.concatenate(tiles[::-1], axis=0)
        rows = pl.ds(pl.multiple_of(group * width, width), width)
        left = jnp.concatenate([signal[rows, lanes_at(first + i + 1, blocks)] for i in range(window)], axis=0)
        result = jnp.dot(left, matrix, preferred_element_type=f32)
        for i in range(window):
            long_part[rows, i * LANES : (i + 1) * LANES] = result[i * width : (i + 1) * width]
        return carry

    lax.fori_loop(0, groups, one_group, 0, unroll=2)
    own = lanes_at(first, window)
    mixed = columns_ref[:, 9:10] * exact[:, own] + long_part[...]
    mixed_ref[...] = mixed
    queries = expand(tap_weights(taps_ref, table_ref, 0), hot[:, lanes_at(first, local_blocks)])
    hidden_ref[...] = jnp.transpose(queries * mixed[:, :local_rows]).astype(bf16)


def backward_kernel(shards, me_ref, *refs):
    ids_slots, filter_slots, grad_slots = refs[:shards], refs[shards : 2 * shards], refs[2 * shards : 3 * shards]
    table_ref, taps_ref, columns_ref, mixed_ref, out_ref = refs[3 * shards : 3 * shards + 5]
    ids_all, hot, filters, grads, signal, exact, long_part = refs[3 * shards + 5 :]
    me = me_ref[0]
    groups, local_rows = filter_slots[0].shape
    channels = table_ref.shape[2]
    width = channels // groups
    local_blocks = local_rows // LANES
    blocks = shards * local_blocks
    length = blocks * LANES
    window = local_blocks + 1
    taps = taps_ref.shape[0]

    for step in range(shards):
        place = lanes_at(jnp.bitwise_xor(me, step) * local_blocks, local_blocks)
        ids_all[:, place] = ids_slots[step][...]
        filters[:, place] = filter_slots[step][...]
        grads[:, place] = grad_slots[step][...]
    grads[:, length:] = jnp.zeros((channels, LANES), bf16)
    marks = one_hot(ids_all[...], taps)
    hot[:, :length] = jnp.concatenate([marks, marks], axis=0).astype(bf16)
    hot[:, length:] = jnp.zeros((hot.shape[0], LANES), bf16)

    signal[:, length:] = jnp.zeros((channels, length + LANES), bf16)
    exact[:, length:] = jnp.zeros((channels, LANES), f32)
    query_weights = tap_weights(taps_ref, table_ref, 0)
    for start in range(0, channels, LANES):
        rows = slice(start, start + LANES)
        mixed_grad = expand(query_weights[:, rows], hot[:, :length]) * grads[rows, :length].astype(f32)
        exact[rows, :length] = mixed_grad
        signal[rows, :length] = mixed_grad.astype(bf16)

    first = me * local_blocks

    def one_group(group, carry):
        tiles = toeplitz_tiles(filters[pl.ds(group, 1), :], blocks)
        matrix = jnp.concatenate(tiles, axis=1)
        rows = pl.ds(pl.multiple_of(group * width, width), width)
        left = jnp.concatenate([signal[rows, lanes_at(first + i, blocks)] for i in range(window)], axis=0)
        result = lax.dot_general(left, matrix, (((1,), (1,)), ((), ())), preferred_element_type=f32)
        for i in range(window):
            long_part[rows, i * LANES : (i + 1) * LANES] = result[i * width : (i + 1) * width]
        return carry

    lax.fori_loop(0, groups, one_group, 0, unroll=2)
    own = lanes_at(first, window)
    mixture_grad = columns_ref[:, 9:10] * exact[:, own] + long_part[...]
    span = window * LANES
    for part in range(3):
        if part == 0:
            feature_grad = grads[:, own].astype(f32) * mixed_ref[...]
        else:
            other = expand(tap_weights(taps_ref, table_ref, 3 - part), hot[:, own])
            feature_grad = mixture_grad * other
        total = columns_ref[:, part : part + 1] * feature_grad
        for tap in range(1, taps):
            column = 3 * tap + part
            total = total + columns_ref[:, column : column + 1] * pltpu.roll(feature_grad, span - tap, axis=1)
        out_ref[part] = jnp.transpose(total[:, :local_rows]).astype(bf16)


def in_vmem(count):
    return [pl.BlockSpec(memory_space=pltpu.VMEM)] * count


def run_forward(me, ids, filters, table, taps, columns):
    shards = len(ids)
    groups, local_rows = filters[0].shape
    channels = table.shape[2]
    length = shards * local_rows
    span = local_rows + LANES
    rows = 2 * taps.shape[0] * IDS
    return pl.pallas_call(
        functools.partial(forward_kernel, shards),
        out_shape=(
            jax.ShapeDtypeStruct((local_rows, channels), bf16),
            jax.ShapeDtypeStruct((channels, span), f32),
        ),
        in_specs=[pl.BlockSpec(memory_space=pltpu.SMEM)] + in_vmem(2 * shards + 3),
        out_specs=tuple(in_vmem(2)),
        scratch_shapes=[
            pltpu.VMEM((1, length), jnp.int32),
            pltpu.VMEM((rows, length + LANES), bf16),
            pltpu.VMEM((groups, length), f32),
            pltpu.VMEM((channels, 2 * length + LANES), bf16),
            pltpu.VMEM((channels, length + LANES), f32),
            pltpu.VMEM((channels, span), f32),
        ],
        compiler_params=pltpu.CompilerParams(vmem_limit_bytes=VMEM_BYTES),
        cost_estimate=pl.CostEstimate(flops=20_000_000_000, bytes_accessed=4_000_000, transcendentals=0),
        name="forward_conv",
    )(me, *ids, *filters, table, taps, columns)


def run_backward(me, ids, filters, grads, table, taps, columns, mixed):
    shards = len(ids)
    groups, local_rows = filters[0].shape
    channels = table.shape[2]
    length = shards * local_rows
    span = local_rows + LANES
    rows = 2 * taps.shape[0] * IDS
    return pl.pallas_call(
        functools.partial(backward_kernel, shards),
        out_shape=jax.ShapeDtypeStruct((3, local_rows, channels), bf16),
        in_specs=[pl.BlockSpec(memory_space=pltpu.SMEM)] + in_vmem(3 * shards + 4),
        out_specs=pl.BlockSpec(memory_space=pltpu.VMEM),
        scratch_shapes=[
            pltpu.VMEM((1, length), jnp.int32),
            pltpu.VMEM((rows, length + LANES), bf16),
            pltpu.VMEM((groups, length), f32),
            pltpu.VMEM((channels, length + LANES), bf16),
            pltpu.VMEM((channels, 2 * length + LANES), bf16),
            pltpu.VMEM((channels, length + LANES), f32),
            pltpu.VMEM((channels, span), f32),
        ],
        compiler_params=pltpu.CompilerParams(vmem_limit_bytes=VMEM_BYTES),
        cost_estimate=pl.CostEstimate(flops=20_000_000_000, bytes_accessed=4_000_000, transcendentals=0),
        name="backward_conv",
    )(me, *ids, *filters, *grads, table, taps, columns, mixed)


def exchange(value, step):
    count = lax.axis_size("ctx")
    return lax.ppermute(value, "ctx", [(i, i ^ step) for i in range(count)])


def gather_ctx(value):
    return [value] + [exchange(value, step) for step in range(1, lax.axis_size("ctx"))]


def to_sibling(value):
    count = lax.axis_size("tp")
    return lax.ppermute(value, "tp", [(i, i ^ 1) for i in range(count)])


def along_chain(value, direction, senders):
    pairs = [(2 * chip + core, 2 * (chip + direction) + core) for chip in senders for core in range(2)]
    return lax.ppermute(value, "tp", pairs)


def chain_reduce_scatter(own):
    chips = own.shape[0]
    chip = lax.axis_index("tp") // 2
    right = left = None
    for step in range(1, chips):
        to_right = own[jnp.clip(chips + chip - step, 0, chips - 1)]
        to_left = own[jnp.clip(chip + step - chips, 0, chips - 1)]
        if right is not None:
            to_right = to_right + right.astype(f32)
            to_left = to_left + left.astype(f32)
        right = along_chain(to_right.astype(bf16), 1, range(0, step))
        left = along_chain(to_left.astype(bf16), -1, range(chips - step, chips))
    return own[chip] + right.astype(f32) + left.astype(f32)


def chain_all_gather(block, chips):
    chip = lax.axis_index("tp") // 2
    from_left, from_right = [], []
    right = left = block
    for step in range(1, chips):
        right = along_chain(right, 1, range(step - 1, chips - 1))
        left = along_chain(left, -1, range(1, chips - step + 1))
        from_left.append(right)
        from_right.append(left)
    line = jnp.concatenate(from_left[::-1] + [block] + from_right, axis=0)
    rows = block.shape[0]
    return lax.dynamic_slice_in_dim(line, (chips - 1 - chip) * rows, chips * rows, axis=0)


def body(
    token_ids,
    embed_table,
    norm_gain,
    input_weight,
    short_weight,
    filters,
    skip_gain,
    output_weight,
    output_grad,
):
    shards = lax.axis_size("ctx")
    chips = lax.axis_size("tp") // 2
    me = lax.axis_index("ctx")
    core = lax.axis_index("tp") % 2
    chip = lax.axis_index("tp") // 2
    local_rows = token_ids.shape[0]
    width, channels = output_weight.shape
    me_array = jnp.reshape(me, (1,)).astype(jnp.int32)

    ids = [jnp.reshape(slot, (1, local_rows)) for slot in gather_ctx(token_ids)]
    filter_slots = gather_ctx(filters)

    hidden_grad = lax.dot_general(
        output_weight, output_grad, (((0,), (1,)), ((), ())), preferred_element_type=f32
    ).astype(bf16)
    grad_slots = gather_ctx(hidden_grad)

    letters = lax.slice_in_dim(embed_table, FIRST_ID, FIRST_ID + IDS, axis=0)
    letter_values = letters.astype(f32)
    inverse_rms = lax.rsqrt(jnp.mean(letter_values * letter_values, axis=-1, keepdims=True) + 1e-06)
    normed = (letter_values * inverse_rms * norm_gain).astype(bf16)
    table = jnp.einsum("qd,djc->jqc", normed, input_weight, preferred_element_type=f32)

    taps = short_weight.shape[0]
    columns = jnp.transpose(
        jnp.concatenate([short_weight.reshape(3 * taps, channels), skip_gain[None, :]], axis=0)
    )
    hidden, mixed = run_forward(me_array, ids, filter_slots, table, short_weight, columns)

    half = width // 2
    theirs = lax.dynamic_slice_in_dim(output_weight, (1 - core) * half, half, axis=0)
    mine = lax.dynamic_slice_in_dim(output_weight, core * half, half, axis=0)
    contract = (((1,), (1,)), ((), ()))
    received = to_sibling(lax.dot_general(hidden, theirs, contract, preferred_element_type=f32).astype(bf16))
    partial_out = lax.dot_general(hidden, mine, contract, preferred_element_type=f32) + received.astype(f32)
    block_rows = local_rows // chips
    own_out = chain_reduce_scatter(partial_out.reshape(chips, block_rows, half))
    own_ids = lax.dynamic_slice_in_dim(token_ids, chip * block_rows, block_rows, axis=0)
    own_hot = (own_ids[:, None] == jnp.arange(FIRST_ID, FIRST_ID + IDS)[None, :]).astype(bf16)
    own_letters = lax.dynamic_slice_in_dim(letters, core * half, half, axis=1)
    own_tokens = jnp.dot(own_hot, own_letters, preferred_element_type=f32)
    final_block = (own_tokens + own_out).astype(bf16)

    projection_grad = run_backward(
        me_array, ids, filter_slots, grad_slots, table, short_weight, columns, mixed
    )
    split_rows = projection_grad.reshape(3, chips, 2, local_rows // (2 * chips), channels)

    def input_part(which):
        rows = lax.dynamic_index_in_dim(split_rows, which, axis=2, keepdims=False)
        rows = rows.reshape(3, local_rows // 2, channels)
        return jnp.einsum("jtc,djc->td", rows, input_weight, preferred_element_type=f32)

    received_grad = to_sibling(input_part(1 - core).astype(bf16))
    partial_grad = input_part(core) + received_grad.astype(f32)
    normed_grad = chain_reduce_scatter(partial_grad.reshape(chips, local_rows // (2 * chips), width))

    my_half = chain_all_gather(final_block, chips)
    other_half = to_sibling(my_half)
    block_output = jnp.where(
        core == 0,
        jnp.concatenate([my_half, other_half], axis=1),
        jnp.concatenate([other_half, my_half], axis=1),
    )

    share = width // shards
    late_grad, late_hidden = lax.optimization_barrier((output_grad, hidden))
    hidden_slots = gather_ctx(late_hidden)
    output_slots = []
    for step in range(shards):
        piece = lax.dynamic_slice_in_dim(late_grad, jnp.bitwise_xor(me, step) * share, share, axis=1)
        output_slots.append(piece if step == 0 else exchange(piece, step))
    output_weight_grad = lax.dot_general(
        jnp.concatenate(output_slots, axis=0),
        jnp.concatenate(hidden_slots, axis=0),
        (((0,), (0,)), ((), ())),
        preferred_element_type=f32,
    )
    return (block_output, output_weight_grad, jnp.transpose(projection_grad, (1, 0, 2)), normed_grad)


def solution(mesh):
    in_specs = (
        P("ctx"),
        P(),
        P(),
        P(None, None, "tp"),
        P(None, None, "tp"),
        P("tp", "ctx"),
        P("tp"),
        P(None, "tp"),
        P("ctx", None),
    )
    out_specs = (P("ctx", None), P("ctx", "tp"), P("ctx", None, "tp"), P(("ctx", "tp"), None))
    return jax.shard_map(body, mesh=mesh, in_specs=in_specs, out_specs=out_specs, check_vma=False)
```

```python
import functools

import jax
import jax.numpy as jnp
from jax import lax
from jax.experimental import pallas as pl
from jax.experimental.pallas import tpu as pltpu
from jax.sharding import PartitionSpec as P

LANES = 128
FIRST_ID = 64
IDS = 32
VMEM_BYTES = 56 * 1024 * 1024
f32 = jnp.float32
bf16 = jnp.bfloat16
CONTRACT_LAST = (((1,), (1,)), ((), ()))


def one_hot(ids, taps):
    length = ids.shape[1]
    lane = lax.broadcasted_iota(jnp.int32, (1, length), 1)
    code = lax.broadcasted_iota(jnp.int32, (IDS, length), 0) + FIRST_ID
    rows = []
    for tap in range(taps):
        moved = ids if tap == 0 else jnp.where(lane < tap, 0, pltpu.roll(ids, tap, axis=1))
        rows.append(jnp.where(code == moved, 1.0, 0.0))
    return jnp.concatenate(rows, axis=0)


def tap_weights(taps_ref, table_ref, part):
    table = table_ref[part]
    value = jnp.concatenate([taps_ref[i, part][None, :] * table for i in range(taps_ref.shape[0])], axis=0)
    high = value.astype(bf16).astype(f32)
    return jnp.concatenate([high, value - high], axis=0).astype(bf16)


def expand(weights, hot):
    return lax.dot_general(weights, hot, (((0,), (0,)), ((), ())), preferred_element_type=f32)


def toeplitz_tiles(row, blocks, mirrored):
    sub = lax.broadcasted_iota(jnp.int32, (LANES, LANES), 0)
    lane = lax.broadcasted_iota(jnp.int32, (LANES, LANES), 1)
    keep = lane <= sub if mirrored else lane >= sub
    before = jnp.zeros((LANES, LANES), f32)
    tiles = []
    for q in range(blocks):
        part = jnp.broadcast_to(row[:, LANES * q : LANES * (q + 1)], (LANES, LANES))
        turned = pltpu.roll(part, 1 if mirrored else 0, 1, stride=1, stride_axis=0)
        tiles.append(jnp.where(keep, turned, before).astype(bf16))
        before = turned
    return tiles


def reverse_blocks(value):
    sub = lax.broadcasted_iota(jnp.int32, (LANES, LANES), 0)
    lane = lax.broadcasted_iota(jnp.int32, (LANES, LANES), 1)
    mirror = jnp.where(sub + lane == LANES - 1, 1.0, 0.0).astype(bf16)
    blocks = [value[:, start : start + LANES].astype(bf16) for start in range(0, value.shape[1], LANES)]
    return jnp.concatenate([jnp.dot(block, mirror, preferred_element_type=f32) for block in blocks], axis=1)


def lanes_at(block, count):
    return pl.ds(pl.multiple_of(block * LANES, LANES), count * LANES)


def channel_columns(taps_ref, skip_ref):
    taps = taps_ref.shape[0]
    rows = [taps_ref[i] for i in range(taps)] + [skip_ref[...][None, :]]
    channels = skip_ref.shape[0]
    rows.append(jnp.zeros((LANES - 3 * taps - 1, channels), f32))
    return jnp.transpose(jnp.concatenate(rows, axis=0))


def place_slots(me, local_blocks, slots, store):
    for step, slot in enumerate(slots):
        store(lanes_at(jnp.bitwise_xor(me, step) * local_blocks, local_blocks), slot)


def start_rows(source_ref, start, held, arrived):
    copies = []
    chunk = held.shape[0] // arrived.shape[0]
    for index in range(arrived.shape[0]):
        rows = pl.ds(pl.multiple_of(start + index * chunk, chunk), chunk)
        copies.append(
            pltpu.make_async_copy(source_ref.at[rows], held.at[index * chunk : (index + 1) * chunk], arrived.at[index])
        )
        copies[-1].start()
    return copies


def project(hidden, copies, weight, out_ref):
    chunk = weight.shape[0] // len(copies)
    for index, copy in enumerate(copies):
        rows = slice(index * chunk, (index + 1) * chunk)
        copy.wait()
        value = lax.dot_general(hidden, weight[rows], CONTRACT_LAST, preferred_element_type=f32)
        out_ref[:, rows] = value.astype(out_ref.dtype)


def own_part_kernel(core_ref, hidden_ref, last_ref, out_ref, last, arrived):
    copies = start_rows(last_ref, core_ref[0] * last.shape[0], last, arrived)
    project(hidden_ref[...], copies, last, out_ref)


def assemble_kernel(chip_ref, core_ref, *refs):
    out_ref = refs[-1]
    chips = (len(refs) - 1) // 2
    rows, columns = refs[0].shape
    for index in range(2 * chips):
        place = jnp.bitwise_xor(chip_ref[0], index % chips)
        side = core_ref[0] if index < chips else 1 - core_ref[0]
        at = (pl.ds(pl.multiple_of(place * rows, rows), rows), pl.ds(pl.multiple_of(side * columns, columns), columns))
        out_ref[at] = refs[index][...]


def forward_kernel(shards, me_ref, core_ref, *refs):
    slots = refs[:shards]
    letters_ref, gain_ref, weight_ref, taps_ref, skip_ref, last_ref = refs[shards : shards + 6]
    hidden_ref, mixed_ref, table_ref, theirs_ref = refs[shards + 6 : shards + 10]
    normed, hot, filters, matrices, signal, exact, long_part, weight, arrived, last, last_arrived = refs[shards + 10 :]
    groups = filters.shape[0]
    local_rows = slots[0].shape[1]
    channels = table_ref.shape[2]
    width = channels // groups
    local_blocks = local_rows // LANES
    blocks = shards * local_blocks
    length = blocks * LANES
    window = local_blocks + 1
    chunks = arrived.shape[0]
    chunk = weight.shape[1] // chunks
    taps = taps_ref.shape[0]
    me = me_ref[0]
    first = me * local_blocks

    copies = []
    for index in range(chunks):
        rows = slice(index * chunk, (index + 1) * chunk)
        copies.append(pltpu.make_async_copy(weight_ref.at[:, rows], weight.at[:, rows], arrived.at[index]))
        copies[-1].start()
    last_copies = start_rows(last_ref, (1 - core_ref[0]) * last.shape[0], last, last_arrived)
    for index, slot in enumerate(slots):
        place = lanes_at(jnp.bitwise_xor(me, index) * local_blocks, local_blocks)
        filters[:, place] = slot[:groups]
        exact[0:1, place] = slot[groups : groups + 1]
    marks = one_hot(exact[0:1, :length].astype(jnp.int32), taps)
    hot[:, :length] = jnp.concatenate([marks, marks], axis=0).astype(bf16)
    hot[:, length:] = jnp.zeros((hot.shape[0], LANES), bf16)
    signal[:, :length] = jnp.zeros((channels, length), bf16)
    signal[:, 2 * length :] = jnp.zeros((channels, LANES), bf16)
    exact[:, length:] = jnp.zeros((channels, LANES), f32)
    values = letters_ref[...].astype(f32)
    inverse = lax.rsqrt(jnp.mean(values * values, axis=-1, keepdims=True) + 1e-06)
    normed[...] = (values * inverse * gain_ref[...][None, :]).astype(bf16)

    def one_matrix(group, carry):
        tiles = toeplitz_tiles(filters[pl.ds(group, 1), :], blocks, False)
        for q in range(blocks):
            matrices[group, (blocks - 1 - q) * LANES : (blocks - q) * LANES] = tiles[q]
        return carry

    for index in range(chunks):
        lax.fori_loop(index * groups // chunks, (index + 1) * groups // chunks, one_matrix, 0)
        rows = slice(index * chunk, (index + 1) * chunk)
        copies[index].wait()
        for part in range(3):
            term = jnp.dot(normed[:, rows], weight[part, rows], preferred_element_type=f32)
            table_ref[part] = term if index == 0 else table_ref[part] + term

    key_weights = tap_weights(taps_ref, table_ref, 1)
    value_weights = tap_weights(taps_ref, table_ref, 2)
    for start in range(0, channels, LANES):
        rows = slice(start, start + LANES)
        mixture = expand(key_weights[:, rows], hot[:, :length]) * expand(value_weights[:, rows], hot[:, :length])
        exact[rows, :length] = mixture
        signal[rows, length : 2 * length] = mixture.astype(bf16)

    def one_group(group, carry):
        rows = pl.ds(pl.multiple_of(group * width, width), width)
        left = jnp.concatenate([signal[rows, lanes_at(first + i + 1, blocks)] for i in range(window)], axis=0)
        result = jnp.dot(left, matrices[group], preferred_element_type=f32)
        for i in range(window):
            long_part[rows, i * LANES : (i + 1) * LANES] = result[i * width : (i + 1) * width]
        return carry

    lax.fori_loop(0, groups, one_group, 0, unroll=4)
    columns = channel_columns(taps_ref, skip_ref)
    mixed = columns[:, 3 * taps : 3 * taps + 1] * exact[:, lanes_at(first, window)] + long_part[...]
    mixed_ref[...] = mixed
    queries = expand(tap_weights(taps_ref, table_ref, 0), hot[:, lanes_at(first, local_blocks)])
    hidden = jnp.transpose(queries * mixed[:, :local_rows]).astype(bf16)
    hidden_ref[...] = hidden
    project(hidden, last_copies, last, theirs_ref)


def backward_kernel(shards, me_ref, *refs):
    slots, grad_slots = refs[:shards], refs[shards : 2 * shards]
    table_ref, taps_ref, skip_ref, mixed_ref, out_ref = refs[2 * shards : 2 * shards + 5]
    hot, filters, grads, signal, exact, long_part = refs[2 * shards + 5 :]
    me = me_ref[0]
    groups = filters.shape[0]
    local_rows = slots[0].shape[1]
    channels = table_ref.shape[2]
    width = channels // groups
    local_blocks = local_rows // LANES
    blocks = shards * local_blocks
    length = blocks * LANES
    window = local_blocks + 1
    taps = taps_ref.shape[0]

    for step in range(shards):
        place = lanes_at(jnp.bitwise_xor(me, step) * local_blocks, local_blocks)
        exact[0:1, place] = slots[step][groups : groups + 1]
        filters[:, place] = reverse_blocks(slots[step][:groups])
        grads[:, place] = grad_slots[step][...]
    grads[:, length:] = jnp.zeros((channels, LANES), bf16)
    marks = one_hot(exact[0:1, :length].astype(jnp.int32), taps)
    hot[:, :length] = jnp.concatenate([marks, marks], axis=0).astype(bf16)
    hot[:, length:] = jnp.zeros((hot.shape[0], LANES), bf16)

    signal[:, length:] = jnp.zeros((channels, length + LANES), bf16)
    exact[:, length:] = jnp.zeros((channels, LANES), f32)
    query_weights = tap_weights(taps_ref, table_ref, 0)
    for start in range(0, channels, LANES):
        rows = slice(start, start + LANES)
        mixed_grad = expand(query_weights[:, rows], hot[:, :length]) * grads[rows, :length].astype(f32)
        exact[rows, :length] = mixed_grad
        signal[rows, :length] = mixed_grad.astype(bf16)

    first = me * local_blocks

    def one_group(group, carry):
        matrix = jnp.concatenate(toeplitz_tiles(filters[pl.ds(group, 1), :], blocks, True), axis=0)
        rows = pl.ds(pl.multiple_of(group * width, width), width)
        left = jnp.concatenate([signal[rows, lanes_at(first + i, blocks)] for i in range(window)], axis=0)
        result = jnp.dot(left, matrix, preferred_element_type=f32)
        for i in range(window):
            long_part[rows, i * LANES : (i + 1) * LANES] = result[i * width : (i + 1) * width]
        return carry

    lax.fori_loop(0, groups, one_group, 0, unroll=4)
    own = lanes_at(first, window)
    columns = channel_columns(taps_ref, skip_ref)
    mixture_grad = columns[:, 3 * taps : 3 * taps + 1] * exact[:, own] + long_part[...]
    span = window * LANES
    for part in range(3):
        if part == 0:
            feature_grad = grads[:, own].astype(f32) * mixed_ref[...]
        else:
            other = expand(tap_weights(taps_ref, table_ref, 3 - part), hot[:, own])
            feature_grad = mixture_grad * other
        total = columns[:, part : part + 1] * feature_grad
        for tap in range(1, taps):
            column = 3 * tap + part
            total = total + columns[:, column : column + 1] * pltpu.roll(feature_grad, span - tap, axis=1)
        out_ref[part] = jnp.transpose(total[:, :local_rows]).astype(bf16)


def hidden_grad_kernel(grad_ref, weight_ref, out_ref, grad, weight, total, arrived):
    chunks = arrived.shape[0] // 2
    chunk = weight.shape[0] // chunks
    copies = []
    for index in range(chunks):
        part = slice(index * chunk, (index + 1) * chunk)
        copies.append(pltpu.make_async_copy(grad_ref.at[:, part], grad.at[:, part], arrived.at[2 * index]))
        copies.append(pltpu.make_async_copy(weight_ref.at[part], weight.at[part], arrived.at[2 * index + 1]))
    for copy in copies:
        copy.start()
    for index in range(chunks):
        part = slice(index * chunk, (index + 1) * chunk)
        copies[2 * index].wait()
        copies[2 * index + 1].wait()
        term = jnp.dot(grad[:, part], weight[part], preferred_element_type=f32)
        total[...] = term if index == 0 else total[...] + term
    out_ref[...] = jnp.transpose(total[...]).astype(bf16)


def input_grad_kernel(chips, start, core_ref, *refs):
    grad_ref, weight_ref, theirs_ref, mine_ref, weight, total, arrived = refs
    chunks = arrived.shape[0]
    chunk = weight.shape[1] // chunks
    copies = []
    for index in range(chunks):
        rows = slice(index * chunk, (index + 1) * chunk)
        source = weight_ref.at[:, start + index * chunk : start + (index + 1) * chunk]
        copies.append(pltpu.make_async_copy(source, weight.at[:, rows], arrived.at[index]))
        copies[-1].start()
    core = core_ref[0]
    rows = total.shape[0] // (2 * chips)

    def half(which):
        starts = [pl.multiple_of((2 * chip + which) * rows, 8) for chip in range(chips)]
        return jnp.concatenate([total[pl.ds(start, rows), :] for start in starts], axis=0)

    for index in range(chunks):
        part_rows = slice(index * chunk, (index + 1) * chunk)
        copies[index].wait()
        value = None
        for part in range(3):
            term = lax.dot_general(
                grad_ref[part], weight[part, part_rows], CONTRACT_LAST, preferred_element_type=f32
            )
            value = term if value is None else value + term
        total[...] = value
        mine_ref[:, part_rows] = half(core)
        theirs_ref[:, part_rows] = half(1 - core).astype(bf16)


def in_vmem(count):
    return [pl.BlockSpec(memory_space=pltpu.VMEM)] * count


SMEM_SPEC = pl.BlockSpec(memory_space=pltpu.SMEM)
ANY_SPEC = pl.BlockSpec(memory_space=pl.ANY)
VMEM_SPEC = pl.BlockSpec(memory_space=pltpu.VMEM)
CHUNKS = 8


def params():
    return pltpu.CompilerParams(vmem_limit_bytes=VMEM_BYTES)


LARGE_COST = pl.CostEstimate(flops=20_000_000_000, bytes_accessed=10_000_000, transcendentals=0)
SMALL_COST = pl.CostEstimate(flops=1000, bytes_accessed=1000, transcendentals=0)


def run_own_part(core, hidden, output_weight):
    half = output_weight.shape[0] // 2
    return pl.pallas_call(
        own_part_kernel,
        out_shape=jax.ShapeDtypeStruct((hidden.shape[0], half), f32),
        in_specs=[SMEM_SPEC, VMEM_SPEC, ANY_SPEC],
        out_specs=VMEM_SPEC,
        scratch_shapes=[pltpu.VMEM((half, hidden.shape[1]), bf16), pltpu.SemaphoreType.DMA((4,))],
        compiler_params=params(),
        cost_estimate=SMALL_COST,
        name="own_part",
    )(core, hidden, output_weight)


def run_assemble(chip, core, own, theirs):
    chips = len(own)
    rows, columns = own[0].shape
    return pl.pallas_call(
        assemble_kernel,
        out_shape=jax.ShapeDtypeStruct((chips * rows, 2 * columns), bf16),
        in_specs=[SMEM_SPEC, SMEM_SPEC] + in_vmem(2 * len(own)),
        out_specs=VMEM_SPEC,
        compiler_params=params(),
        cost_estimate=SMALL_COST,
        name="assemble",
    )(chip, core, *own, *theirs)


def run_forward(me, core, slots, embed_table, norm_gain, weight, taps, skip_gain, output_weight):
    shards = len(slots)
    local_rows = slots[0].shape[1]
    _, width, channels = weight.shape
    groups = slots[0].shape[0] - 8
    length = shards * local_rows
    span = local_rows + LANES
    return pl.pallas_call(
        functools.partial(forward_kernel, shards),
        grid=(1,),
        out_shape=(
            jax.ShapeDtypeStruct((local_rows, channels), bf16),
            jax.ShapeDtypeStruct((channels, span), f32),
            jax.ShapeDtypeStruct((3, IDS, channels), f32),
            jax.ShapeDtypeStruct((local_rows, width // 2), bf16),
        ),
        in_specs=[SMEM_SPEC, SMEM_SPEC]
        + in_vmem(shards)
        + [pl.BlockSpec((IDS, width), lambda step: (FIRST_ID // IDS, 0)), VMEM_SPEC, ANY_SPEC, VMEM_SPEC, VMEM_SPEC]
        + [ANY_SPEC],
        out_specs=tuple(in_vmem(4)),
        scratch_shapes=[
            pltpu.VMEM((IDS, width), bf16),
            pltpu.VMEM((2 * taps.shape[0] * IDS, length + LANES), bf16),
            pltpu.VMEM((groups, length), f32),
            pltpu.VMEM((groups, length, LANES), bf16),
            pltpu.VMEM((channels, 2 * length + LANES), bf16),
            pltpu.VMEM((channels, length + LANES), f32),
            pltpu.VMEM((channels, span), f32),
            pltpu.VMEM(weight.shape, bf16),
            pltpu.SemaphoreType.DMA((CHUNKS,)),
            pltpu.VMEM((width // 2, channels), bf16),
            pltpu.SemaphoreType.DMA((4,)),
        ],
        compiler_params=params(),
        cost_estimate=LARGE_COST,
        name="forward_conv",
    )(me, core, *slots, embed_table, norm_gain, weight, taps, skip_gain, output_weight)


def run_backward(me, slots, grads, table, taps, skip_gain, mixed):
    shards = len(slots)
    local_rows = slots[0].shape[1]
    channels = table.shape[2]
    groups = slots[0].shape[0] - 8
    length = shards * local_rows
    span = local_rows + LANES
    return pl.pallas_call(
        functools.partial(backward_kernel, shards),
        out_shape=jax.ShapeDtypeStruct((3, local_rows, channels), bf16),
        in_specs=[SMEM_SPEC] + in_vmem(2 * shards + 4),
        out_specs=VMEM_SPEC,
        scratch_shapes=[
            pltpu.VMEM((2 * taps.shape[0] * IDS, length + LANES), bf16),
            pltpu.VMEM((groups, length), f32),
            pltpu.VMEM((channels, length + LANES), bf16),
            pltpu.VMEM((channels, 2 * length + LANES), bf16),
            pltpu.VMEM((channels, length + LANES), f32),
            pltpu.VMEM((channels, span), f32),
        ],
        compiler_params=params(),
        cost_estimate=LARGE_COST,
        name="backward_conv",
    )(me, *slots, *grads, table, taps, skip_gain, mixed)


def run_hidden_grad(output_grad, output_weight):
    rows, width = output_grad.shape
    channels = output_weight.shape[1]
    return pl.pallas_call(
        hidden_grad_kernel,
        out_shape=jax.ShapeDtypeStruct((channels, rows), bf16),
        in_specs=[ANY_SPEC, ANY_SPEC],
        out_specs=VMEM_SPEC,
        scratch_shapes=[
            pltpu.VMEM((rows, width), bf16),
            pltpu.VMEM((width, channels), bf16),
            pltpu.VMEM((rows, channels), f32),
            pltpu.SemaphoreType.DMA((2 * CHUNKS,)),
        ],
        compiler_params=params(),
        cost_estimate=SMALL_COST,
        name="hidden_grad",
    )(output_grad, output_weight)


def run_input_grad(side, core, chips, projection_grad, weight):
    _, rows, channels = projection_grad.shape
    width = weight.shape[1] // 2
    return pl.pallas_call(
        functools.partial(input_grad_kernel, chips, side * width),
        out_shape=(
            jax.ShapeDtypeStruct((rows // 2, width), bf16),
            jax.ShapeDtypeStruct((rows // 2, width), f32),
        ),
        in_specs=[SMEM_SPEC, VMEM_SPEC, ANY_SPEC],
        out_specs=(VMEM_SPEC, VMEM_SPEC),
        scratch_shapes=[
            pltpu.VMEM((3, width, channels), bf16),
            pltpu.VMEM((rows, width // 4), f32),
            pltpu.SemaphoreType.DMA((4,)),
        ],
        compiler_params=params(),
        cost_estimate=LARGE_COST,
        name="input_grad",
    )(core, projection_grad, weight)


def ctx_exchange(value, step):
    count = lax.axis_size("ctx")
    return lax.ppermute(value, "ctx", [(i, i ^ step) for i in range(count)])


def gather_ctx(value):
    return [value] + [ctx_exchange(value, step) for step in range(1, lax.axis_size("ctx"))]


def tp_exchange(value, mask):
    count = lax.axis_size("tp")
    return lax.ppermute(value, "tp", [(i, i ^ mask) for i in range(count)])


def together(*values):
    return lax.optimization_barrier(values)


def pick(value, index, axis=0):
    return lax.dynamic_index_in_dim(value, index, axis=axis, keepdims=False)


def scalar_array(value):
    return jnp.reshape(value, (1,)).astype(jnp.int32)


def body(
    token_ids,
    embed_table,
    norm_gain,
    input_weight,
    short_weight,
    filters,
    skip_gain,
    output_weight,
    output_grad,
):
    shards = lax.axis_size("ctx")
    chips = lax.axis_size("tp") // 2
    hops = chips - 1
    me = lax.axis_index("ctx")
    core = lax.axis_index("tp") % 2
    chip = lax.axis_index("tp") // 2
    local_rows = token_ids.shape[0]
    width, channels = output_weight.shape
    me_tie, core_tie, chip_tie = scalar_array(me), scalar_array(core), scalar_array(chip)
    weight = jnp.transpose(input_weight, (1, 0, 2))

    groups = filters.shape[0]
    row_number = lax.broadcasted_iota(jnp.int32, (groups + 8, local_rows), 0)
    packed = jnp.where(
        row_number < groups, jnp.pad(filters, ((0, 8), (0, 0))), token_ids.astype(f32)[None, :]
    )
    slots = gather_ctx(packed)
    hidden_grad = run_hidden_grad(output_grad, output_weight)
    arrived, hidden_grad, me_tie = together(slots[1:], hidden_grad, me_tie)
    slots = [packed] + arrived
    grad_slots = gather_ctx(hidden_grad)

    hidden, mixed, table, for_sibling = run_forward(
        me_tie, core_tie, slots, embed_table, norm_gain, weight, short_weight, skip_gain, output_weight
    )
    for_sibling, hidden, grad_slots = together(for_sibling, hidden, grad_slots)
    half = width // 2
    block_rows = local_rows // chips
    received = tp_exchange(for_sibling, 1)
    mine = run_own_part(core_tie, hidden, output_weight)
    received, mine, me_tie, late_hidden = together(received, mine, me_tie, hidden)
    mine = mine.reshape(chips, block_rows, half)
    received = received.reshape(chips, block_rows, half)

    def out_block(index):
        return pick(mine, index) + pick(received, index).astype(f32)

    order = list(range(2, chips)) + [1]
    first, second = order[: (chips - 1) // 2], order[(chips - 1) // 2 :]
    share = width // shards
    part = share // 2

    def out_sends(steps):
        return [out_block(jnp.bitwise_xor(chip, step)).astype(bf16) for step in steps]

    def ctx_pieces(steps):
        starts = [jnp.bitwise_xor(me, step) * share + core * part for step in steps]
        return [
            jnp.concatenate([lax.dynamic_slice_in_dim(output_grad, start, part, axis=1), late_hidden], axis=1)
            for start in starts
        ]

    ctx_first, ctx_second = range(1, shards // 2 + 1), range(shards // 2 + 1, shards)
    sends, pieces, me_tie = together(out_sends(first), ctx_pieces(ctx_first), me_tie)
    out_arrived = [tp_exchange(value, 2 * step) for step, value in zip(first, sends)]
    ctx_arrived = [ctx_exchange(value, step) for step, value in zip(ctx_first, pieces)]
    projection_grad = run_backward(
        me_tie, slots, grad_slots, table, short_weight, skip_gain, mixed
    )
    sends, pieces = out_sends(second), ctx_pieces(ctx_second)
    out_arrived, ctx_arrived, projection_grad, sends, pieces, core_tie = together(
        out_arrived, ctx_arrived, projection_grad, sends, pieces, core_tie
    )
    out_more = [tp_exchange(value, 2 * step) for step, value in zip(second, sends)]
    ctx_more = [ctx_exchange(value, step) for step, value in zip(ctx_second, pieces)]
    theirs_low, mine_low = run_input_grad(0, core_tie, chips, projection_grad, weight)
    theirs_low, mine_low, core_tie = together(theirs_low, mine_low, core_tie)
    received_low = tp_exchange(theirs_low, 1)
    theirs_high, mine_high = run_input_grad(1, core_tie, chips, projection_grad, weight)
    out_more, ctx_more, received_low, theirs_high, mine_high, core_tie = together(
        out_more, ctx_more, received_low, theirs_high, mine_high, core_tie
    )
    ctx_arrived = ctx_arrived + ctx_more

    received_high = tp_exchange(theirs_high, 1)
    own_ids = lax.dynamic_slice_in_dim(token_ids, chip * block_rows, block_rows, axis=0)
    own_hot = (own_ids[:, None] == jnp.arange(FIRST_ID, FIRST_ID + IDS)[None, :]).astype(bf16)
    own_letters = lax.dynamic_slice(embed_table, (FIRST_ID, core * half), (IDS, half))
    block = jnp.dot(own_hot, own_letters, preferred_element_type=f32) + out_block(chip)
    for value in out_arrived + out_more:
        block = block + value.astype(f32)
    block = block.astype(bf16)
    block, received_high = together(block, received_high)
    line = {step: tp_exchange(block, 2 * step) for step in order[:-1]}
    other_line = {0: tp_exchange(block, 1)}
    line[0] = block
    split = (chips, local_rows // (2 * chips), width)
    total = jnp.concatenate([mine_low, mine_high], axis=1).reshape(split)
    total = total + jnp.concatenate([received_low, received_high], axis=1).reshape(split).astype(f32)

    def halve(value, bit):
        pairs = value.reshape((value.shape[0] // 2, 2) + value.shape[1:])
        which = chip >> bit & 1
        return pick(pairs, which, 1), pick(pairs, 1 - which, 1).astype(bf16)

    levels = chips.bit_length() - 1
    ctx_parts = jnp.concatenate([value[:, :part] for value in ctx_arrived], axis=0)
    for bit in range(levels):
        kept, leaving = halve(total, bit)
        if bit == levels - 1:
            line[1] = tp_exchange(block, 2)
        arriving = tp_exchange(leaving, 2 << bit)
        if bit == 0:
            other_parts = tp_exchange(ctx_parts, 1)
            steps = order[:-1]
            values = [line[step] for step in steps]
            arriving, values, other_parts, line[0], block = together(
                arriving, values, other_parts, line[0], block
            )
            line.update(zip(steps, values))
            for step in steps:
                other_line[step] = tp_exchange(line[step], 1)
        total = kept + arriving.astype(f32)
    other_line[1] = tp_exchange(line[1], 1)

    own_piece = lax.dynamic_slice_in_dim(output_grad, me * share, share, axis=1)
    own_parts = own_piece.reshape(local_rows, 2, part)
    my_columns = jnp.concatenate([pick(own_parts, core, 1), ctx_parts], axis=0)
    other_columns = jnp.concatenate([pick(own_parts, 1 - core, 1), other_parts], axis=0)
    columns = jnp.where(
        core == 0,
        jnp.concatenate([my_columns, other_columns], axis=1),
        jnp.concatenate([other_columns, my_columns], axis=1),
    )
    all_hidden = jnp.concatenate([late_hidden] + [value[:, part:] for value in ctx_arrived], axis=0)
    output_weight_grad = lax.dot_general(
        columns, all_hidden, (((0,), (0,)), ((), ())), preferred_element_type=f32
    )
    block_output = run_assemble(
        chip_tie,
        core_tie,
        [line[step] for step in range(chips)],
        [other_line[step] for step in range(chips)],
    )
    normed_grad = total.reshape(local_rows // (2 * chips), width)
    return (block_output, output_weight_grad, jnp.transpose(projection_grad, (1, 0, 2)), normed_grad)


def solution(mesh):
    in_specs = (
        P("ctx"),
        P(),
        P(),
        P(None, None, "tp"),
        P(None, None, "tp"),
        P("tp", "ctx"),
        P("tp"),
        P(None, "tp"),
        P("ctx", None),
    )
    out_specs = (P("ctx", None), P("ctx", "tp"), P("ctx", None, "tp"), P(("ctx", "tp"), None))
    return jax.shard_map(body, mesh=mesh, in_specs=in_specs, out_specs=out_specs, check_vma=False)
```

```python
import functools

import jax
import jax.numpy as jnp
from jax import lax
from jax.experimental import pallas as pl
from jax.experimental.pallas import tpu as pltpu
from jax.sharding import PartitionSpec as P

LANES = 128
FIRST_ID = 64
IDS = 32
VMEM_BYTES = 56 * 1024 * 1024
f32 = jnp.float32
bf16 = jnp.bfloat16
CONTRACT_LAST = (((1,), (1,)), ((), ()))


def one_hot(ids, taps):
    length = ids.shape[1]
    lane = lax.broadcasted_iota(jnp.int32, (1, length), 1)
    code = lax.broadcasted_iota(jnp.int32, (IDS, length), 0) + FIRST_ID
    rows = []
    for tap in range(taps):
        moved = ids if tap == 0 else jnp.where(lane < tap, 0, pltpu.roll(ids, tap, axis=1))
        rows.append(jnp.where(code == moved, 1.0, 0.0))
    return jnp.concatenate(rows, axis=0)


def tap_weights(taps_ref, table_ref, part):
    table = table_ref[part]
    value = jnp.concatenate([taps_ref[i, part][None, :] * table for i in range(taps_ref.shape[0])], axis=0)
    high = value.astype(bf16).astype(f32)
    return jnp.concatenate([high, value - high], axis=0).astype(bf16)


def expand(weights, hot):
    return lax.dot_general(weights, hot, (((0,), (0,)), ((), ())), preferred_element_type=f32)


def toeplitz_tiles(row, blocks, mirrored):
    sub = lax.broadcasted_iota(jnp.int32, (LANES, LANES), 0)
    lane = lax.broadcasted_iota(jnp.int32, (LANES, LANES), 1)
    keep = lane <= sub if mirrored else lane >= sub
    before = jnp.zeros((LANES, LANES), f32)
    tiles = []
    for q in range(blocks):
        part = jnp.broadcast_to(row[:, LANES * q : LANES * (q + 1)], (LANES, LANES))
        turned = pltpu.roll(part, 1 if mirrored else 0, 1, stride=1, stride_axis=0)
        tiles.append(jnp.where(keep, turned, before).astype(bf16))
        before = turned
    return tiles


def reverse_blocks(value):
    sub = lax.broadcasted_iota(jnp.int32, (LANES, LANES), 0)
    lane = lax.broadcasted_iota(jnp.int32, (LANES, LANES), 1)
    mirror = jnp.where(sub + lane == LANES - 1, 1.0, 0.0).astype(bf16)
    blocks = [value[:, start : start + LANES].astype(bf16) for start in range(0, value.shape[1], LANES)]
    return jnp.concatenate([jnp.dot(block, mirror, preferred_element_type=f32) for block in blocks], axis=1)


def lanes_at(block, count):
    return pl.ds(pl.multiple_of(block * LANES, LANES), count * LANES)


def channel_columns(taps_ref, skip_ref):
    taps = taps_ref.shape[0]
    rows = [taps_ref[i] for i in range(taps)] + [skip_ref[...][None, :]]
    channels = skip_ref.shape[0]
    rows.append(jnp.zeros((LANES - 3 * taps - 1, channels), f32))
    return jnp.transpose(jnp.concatenate(rows, axis=0))


def place_slots(me, local_blocks, slots, store):
    for step, slot in enumerate(slots):
        store(lanes_at(jnp.bitwise_xor(me, step) * local_blocks, local_blocks), slot)


def start_rows(source_ref, start, held, arrived):
    copies = []
    chunk = held.shape[0] // arrived.shape[0]
    for index in range(arrived.shape[0]):
        rows = pl.ds(pl.multiple_of(start + index * chunk, chunk), chunk)
        copies.append(
            pltpu.make_async_copy(source_ref.at[rows], held.at[index * chunk : (index + 1) * chunk], arrived.at[index])
        )
        copies[-1].start()
    return copies


def project(hidden, copies, weight, staged, out_ref, left):
    chunk = weight.shape[0] // len(copies)
    leaving = []
    for index, copy in enumerate(copies):
        rows = slice(index * chunk, (index + 1) * chunk)
        copy.wait()
        value = lax.dot_general(hidden, weight[rows], CONTRACT_LAST, preferred_element_type=f32)
        staged[:, rows] = value.astype(staged.dtype)
        leaving.append(pltpu.make_async_copy(staged.at[:, rows], out_ref.at[:, rows], left.at[index]))
        leaving[-1].start()
    return leaving


def assemble_kernel(steps, chip_ref, core_ref, *refs):
    out_ref = refs[-1]
    rows, columns = refs[0].shape
    for index, step in enumerate(steps + steps):
        place = jnp.bitwise_xor(chip_ref[0], step)
        side = core_ref[0] if index < len(steps) else 1 - core_ref[0]
        at = (pl.ds(pl.multiple_of(place * rows, rows), rows), pl.ds(pl.multiple_of(side * columns, columns), columns))
        out_ref[at] = refs[index][...]


def forward_kernel(shards, me_ref, core_ref, *refs):
    slots = refs[:shards]
    letters_ref, gain_ref, weight_ref, taps_ref, skip_ref, last_ref = refs[shards : shards + 6]
    hidden_ref, mixed_ref, table_ref, theirs_ref, mine_ref = refs[shards + 6 : shards + 11]
    normed, hot, filters, matrices, signal, exact, long_part, weight, arrived, last, last_arrived = refs[shards + 11 : shards + 22]
    own, own_arrived, table, staged, own_staged, left = refs[shards + 22 :]
    groups = filters.shape[0]
    local_rows = slots[0].shape[1]
    channels = table.shape[2]
    width = channels // groups
    local_blocks = local_rows // LANES
    blocks = shards * local_blocks
    length = blocks * LANES
    window = local_blocks + 1
    chunks = arrived.shape[0]
    chunk = weight.shape[1] // chunks
    taps = taps_ref.shape[0]
    me = me_ref[0]
    first = me * local_blocks

    copies = []
    for index in range(chunks):
        rows = slice(index * chunk, (index + 1) * chunk)
        copies.append(pltpu.make_async_copy(weight_ref.at[:, rows], weight.at[:, rows], arrived.at[index]))
        copies[-1].start()
    last_copies = start_rows(last_ref, (1 - core_ref[0]) * last.shape[0], last, last_arrived)
    own_copies = start_rows(last_ref, core_ref[0] * last.shape[0], own, own_arrived)
    for index, slot in enumerate(slots):
        place = lanes_at(jnp.bitwise_xor(me, index) * local_blocks, local_blocks)
        filters[:, place] = slot[:groups]
        exact[0:1, place] = slot[groups : groups + 1]
    marks = one_hot(exact[0:1, :length].astype(jnp.int32), taps)
    hot[:, :length] = jnp.concatenate([marks, marks], axis=0).astype(bf16)
    hot[:, length:] = jnp.zeros((hot.shape[0], LANES), bf16)
    signal[:, :length] = jnp.zeros((channels, length), bf16)
    signal[:, 2 * length :] = jnp.zeros((channels, LANES), bf16)
    exact[:, length:] = jnp.zeros((channels, LANES), f32)
    values = letters_ref[...].astype(f32)
    inverse = lax.rsqrt(jnp.mean(values * values, axis=-1, keepdims=True) + 1e-06)
    normed[...] = (values * inverse * gain_ref[...][None, :]).astype(bf16)

    def one_matrix(group, carry):
        tiles = toeplitz_tiles(filters[pl.ds(group, 1), :], blocks, False)
        for q in range(blocks):
            matrices[group, (blocks - 1 - q) * LANES : (blocks - q) * LANES] = tiles[q]
        return carry

    for index in range(chunks):
        lax.fori_loop(index * groups // chunks, (index + 1) * groups // chunks, one_matrix, 0)
        rows = slice(index * chunk, (index + 1) * chunk)
        copies[index].wait()
        for part in range(3):
            term = jnp.dot(normed[:, rows], weight[part, rows], preferred_element_type=f32)
            table[part] = term if index == 0 else table[part] + term

    table_copy = pltpu.make_async_copy(table, table_ref, left.at[0])
    table_copy.start()
    key_weights = tap_weights(taps_ref, table, 1)
    value_weights = tap_weights(taps_ref, table, 2)
    for start in range(0, channels, LANES):
        rows = slice(start, start + LANES)
        mixture = expand(key_weights[:, rows], hot[:, :length]) * expand(value_weights[:, rows], hot[:, :length])
        exact[rows, :length] = mixture
        signal[rows, length : 2 * length] = mixture.astype(bf16)

    def one_group(group, carry):
        rows = pl.ds(pl.multiple_of(group * width, width), width)
        left = jnp.concatenate([signal[rows, lanes_at(first + i + 1, blocks)] for i in range(window)], axis=0)
        result = jnp.dot(left, matrices[group], preferred_element_type=f32)
        for i in range(window):
            long_part[rows, i * LANES : (i + 1) * LANES] = result[i * width : (i + 1) * width]
        return carry

    lax.fori_loop(0, groups, one_group, 0, unroll=4)
    columns = channel_columns(taps_ref, skip_ref)
    mixed = columns[:, 3 * taps : 3 * taps + 1] * exact[:, lanes_at(first, window)] + long_part[...]
    long_part[...] = mixed
    mixed_copy = pltpu.make_async_copy(long_part, mixed_ref, left.at[1])
    mixed_copy.start()
    queries = expand(tap_weights(taps_ref, table, 0), hot[:, lanes_at(first, local_blocks)])
    hidden = jnp.transpose(queries * mixed[:, :local_rows]).astype(bf16)
    hidden_ref[...] = hidden
    leaving = project(hidden, last_copies, last, staged, theirs_ref, left.at[2:6])
    leaving += project(hidden, own_copies, own, own_staged, mine_ref, left.at[6:])
    for copy in [table_copy, mixed_copy] + leaving:
        copy.wait()


def backward_kernel(shards, me_ref, *refs):
    slots, grad_slots = refs[:shards], refs[shards : 2 * shards]
    table_ref, taps_ref, skip_ref, mixed_ref, out_ref = refs[2 * shards : 2 * shards + 5]
    hot, filters, grads, signal, exact, long_part = refs[2 * shards + 5 :]
    me = me_ref[0]
    groups = filters.shape[0]
    local_rows = slots[0].shape[1]
    channels = table_ref.shape[2]
    width = channels // groups
    local_blocks = local_rows // LANES
    blocks = shards * local_blocks
    length = blocks * LANES
    window = local_blocks + 1
    taps = taps_ref.shape[0]

    for step in range(shards):
        place = lanes_at(jnp.bitwise_xor(me, step) * local_blocks, local_blocks)
        exact[0:1, place] = slots[step][groups : groups + 1]
        filters[:, place] = reverse_blocks(slots[step][:groups])
        grads[:, place] = grad_slots[step][...]
    grads[:, length:] = jnp.zeros((channels, LANES), bf16)
    marks = one_hot(exact[0:1, :length].astype(jnp.int32), taps)
    hot[:, :length] = jnp.concatenate([marks, marks], axis=0).astype(bf16)
    hot[:, length:] = jnp.zeros((hot.shape[0], LANES), bf16)

    signal[:, length:] = jnp.zeros((channels, length + LANES), bf16)
    exact[:, length:] = jnp.zeros((channels, LANES), f32)
    query_weights = tap_weights(taps_ref, table_ref, 0)
    for start in range(0, channels, LANES):
        rows = slice(start, start + LANES)
        mixed_grad = expand(query_weights[:, rows], hot[:, :length]) * grads[rows, :length].astype(f32)
        exact[rows, :length] = mixed_grad
        signal[rows, :length] = mixed_grad.astype(bf16)

    first = me * local_blocks

    def one_group(group, carry):
        matrix = jnp.concatenate(toeplitz_tiles(filters[pl.ds(group, 1), :], blocks, True), axis=0)
        rows = pl.ds(pl.multiple_of(group * width, width), width)
        left = jnp.concatenate([signal[rows, lanes_at(first + i, blocks)] for i in range(window)], axis=0)
        result = jnp.dot(left, matrix, preferred_element_type=f32)
        for i in range(window):
            long_part[rows, i * LANES : (i + 1) * LANES] = result[i * width : (i + 1) * width]
        return carry

    lax.fori_loop(0, groups, one_group, 0, unroll=4)
    own = lanes_at(first, window)
    columns = channel_columns(taps_ref, skip_ref)
    mixture_grad = columns[:, 3 * taps : 3 * taps + 1] * exact[:, own] + long_part[...]
    span = window * LANES
    for part in range(3):
        if part == 0:
            feature_grad = grads[:, own].astype(f32) * mixed_ref[...]
        else:
            other = expand(tap_weights(taps_ref, table_ref, 3 - part), hot[:, own])
            feature_grad = mixture_grad * other
        total = columns[:, part : part + 1] * feature_grad
        for tap in range(1, taps):
            column = 3 * tap + part
            total = total + columns[:, column : column + 1] * pltpu.roll(feature_grad, span - tap, axis=1)
        out_ref[part] = jnp.transpose(total[:, :local_rows]).astype(bf16)


def hidden_grad_kernel(grad_ref, weight_ref, out_ref, grad, weight, total, arrived):
    chunks = arrived.shape[0] // 2
    chunk = weight.shape[0] // chunks
    copies = []
    for index in range(chunks):
        part = slice(index * chunk, (index + 1) * chunk)
        copies.append(pltpu.make_async_copy(grad_ref.at[:, part], grad.at[:, part], arrived.at[2 * index]))
        copies.append(pltpu.make_async_copy(weight_ref.at[part], weight.at[part], arrived.at[2 * index + 1]))
    for copy in copies:
        copy.start()
    for index in range(chunks):
        part = slice(index * chunk, (index + 1) * chunk)
        copies[2 * index].wait()
        copies[2 * index + 1].wait()
        term = jnp.dot(grad[:, part], weight[part], preferred_element_type=f32)
        total[...] = term if index == 0 else total[...] + term
    out_ref[...] = jnp.transpose(total[...]).astype(bf16)


def input_grad_kernel(chips, core_ref, grad_ref, weight_ref, theirs_ref, mine_ref, weight, total, theirs, mine, arrived, left):
    chunks = arrived.shape[0]
    chunk = weight.shape[1] // chunks
    copies = []
    for index in range(chunks):
        columns = slice(index * chunk, (index + 1) * chunk)
        copies.append(pltpu.make_async_copy(weight_ref.at[:, columns], weight.at[:, columns], arrived.at[index]))
        copies[-1].start()
    core = core_ref[0]
    rows = total.shape[0] // (2 * chips)

    def half(which):
        starts = [pl.multiple_of((2 * chip + which) * rows, 8) for chip in range(chips)]
        return jnp.concatenate([total[pl.ds(start, rows), :] for start in starts], axis=0)

    leaving = []
    for index in range(chunks):
        columns = slice(index * chunk, (index + 1) * chunk)
        copies[index].wait()
        value = None
        for part in range(3):
            term = lax.dot_general(
                grad_ref[part], weight[part, columns], CONTRACT_LAST, preferred_element_type=f32
            )
            value = term if value is None else value + term
        total[...] = value
        theirs[:, columns] = half(1 - core).astype(bf16)
        mine[:, columns] = half(core).astype(bf16)
        for slot, (source, target) in enumerate(((theirs, theirs_ref), (mine, mine_ref))):
            copy = pltpu.make_async_copy(source.at[:, columns], target.at[:, columns], left.at[2 * index + slot])
            copy.start()
            leaving.append(copy)
    for copy in leaving:
        copy.wait()


def weight_grad_kernel(shards, me_ref, grad_ref, hidden_ref, *refs):
    slots = refs[: shards - 1]
    out_ref, own, arrived = refs[shards - 1 :]
    share = own.shape[1]
    source = grad_ref.at[:, pl.ds(pl.multiple_of(me_ref[0] * share, share), share)]
    copy = pltpu.make_async_copy(source, own, arrived)
    copy.start()
    chunk = share // 2
    copy.wait()
    for start in range(0, share, chunk):
        columns = slice(start, start + chunk)
        total = expand(own[:, columns], hidden_ref[...])
        for slot in slots:
            total = total + expand(slot[:, columns], slot[:, share:])
        out_ref[columns, :] = total


def in_vmem(count):
    return [pl.BlockSpec(memory_space=pltpu.VMEM)] * count


SMEM_SPEC = pl.BlockSpec(memory_space=pltpu.SMEM)
ANY_SPEC = pl.BlockSpec(memory_space=pl.ANY)
VMEM_SPEC = pl.BlockSpec(memory_space=pltpu.VMEM)
CHUNKS = 8


def params():
    return pltpu.CompilerParams(vmem_limit_bytes=VMEM_BYTES)


LARGE_COST = pl.CostEstimate(flops=20_000_000_000, bytes_accessed=10_000_000, transcendentals=0)
SMALL_COST = pl.CostEstimate(flops=1000, bytes_accessed=1000, transcendentals=0)


def insert_kernel(chip_ref, core_ref, own_ref, theirs_ref, base_ref, out_ref, moved):
    rows, columns = own_ref.shape
    place = pl.ds(pl.multiple_of(jnp.bitwise_xor(chip_ref[0], 1) * rows, rows), rows)
    copies = []
    for index, source in enumerate((own_ref, theirs_ref)):
        side = core_ref[0] if index == 0 else 1 - core_ref[0]
        target = out_ref.at[place, pl.ds(pl.multiple_of(side * columns, columns), columns)]
        copies.append(pltpu.make_async_copy(source, target, moved.at[index]))
        copies[-1].start()
    for copy in copies:
        copy.wait()


def run_insert(chip, core, own, theirs, base):
    return pl.pallas_call(
        insert_kernel,
        out_shape=jax.ShapeDtypeStruct(base.shape, base.dtype),
        in_specs=[SMEM_SPEC, SMEM_SPEC, VMEM_SPEC, VMEM_SPEC, ANY_SPEC],
        out_specs=ANY_SPEC,
        scratch_shapes=[pltpu.SemaphoreType.DMA((2,))],
        input_output_aliases={4: 0},
        compiler_params=params(),
        cost_estimate=SMALL_COST,
        name="insert",
    )(chip, core, own, theirs, base)


def run_assemble(chips, steps, chip, core, own, theirs):
    rows, columns = own[0].shape
    return pl.pallas_call(
        functools.partial(assemble_kernel, steps),
        out_shape=jax.ShapeDtypeStruct((chips * rows, 2 * columns), bf16),
        in_specs=[SMEM_SPEC, SMEM_SPEC] + in_vmem(2 * len(own)),
        out_specs=VMEM_SPEC,
        compiler_params=params(),
        cost_estimate=SMALL_COST,
        name="assemble",
    )(chip, core, *own, *theirs)


def run_forward(me, core, slots, embed_table, norm_gain, weight, taps, skip_gain, output_weight):
    shards = len(slots)
    local_rows = slots[0].shape[1]
    _, width, channels = weight.shape
    groups = slots[0].shape[0] - 8
    length = shards * local_rows
    span = local_rows + LANES
    return pl.pallas_call(
        functools.partial(forward_kernel, shards),
        grid=(1,),
        out_shape=(
            jax.ShapeDtypeStruct((local_rows, channels), bf16),
            jax.ShapeDtypeStruct((channels, span), f32),
            jax.ShapeDtypeStruct((3, IDS, channels), f32),
            jax.ShapeDtypeStruct((local_rows, width // 2), bf16),
            jax.ShapeDtypeStruct((local_rows, width // 2), bf16),
        ),
        in_specs=[SMEM_SPEC, SMEM_SPEC]
        + in_vmem(shards)
        + [pl.BlockSpec((IDS, width), lambda step: (FIRST_ID // IDS, 0)), VMEM_SPEC, ANY_SPEC, VMEM_SPEC, VMEM_SPEC]
        + [ANY_SPEC],
        out_specs=(VMEM_SPEC, ANY_SPEC, ANY_SPEC, ANY_SPEC, ANY_SPEC),
        scratch_shapes=[
            pltpu.VMEM((IDS, width), bf16),
            pltpu.VMEM((2 * taps.shape[0] * IDS, length + LANES), bf16),
            pltpu.VMEM((groups, length), f32),
            pltpu.VMEM((groups, length, LANES), bf16),
            pltpu.VMEM((channels, 2 * length + LANES), bf16),
            pltpu.VMEM((channels, length + LANES), f32),
            pltpu.VMEM((channels, span), f32),
            pltpu.VMEM(weight.shape, bf16),
            pltpu.SemaphoreType.DMA((CHUNKS,)),
            pltpu.VMEM((width // 2, channels), bf16),
            pltpu.SemaphoreType.DMA((4,)),
            pltpu.VMEM((width // 2, channels), bf16),
            pltpu.SemaphoreType.DMA((4,)),
            pltpu.VMEM((3, IDS, channels), f32),
            pltpu.VMEM((local_rows, width // 2), bf16),
            pltpu.VMEM((local_rows, width // 2), bf16),
            pltpu.SemaphoreType.DMA((10,)),
        ],
        compiler_params=params(),
        cost_estimate=LARGE_COST,
        name="forward_conv",
    )(me, core, *slots, embed_table, norm_gain, weight, taps, skip_gain, output_weight)


def run_backward(me, slots, grads, table, taps, skip_gain, mixed):
    shards = len(slots)
    local_rows = slots[0].shape[1]
    channels = table.shape[2]
    groups = slots[0].shape[0] - 8
    length = shards * local_rows
    span = local_rows + LANES
    return pl.pallas_call(
        functools.partial(backward_kernel, shards),
        out_shape=jax.ShapeDtypeStruct((3, local_rows, channels), bf16),
        in_specs=[SMEM_SPEC] + in_vmem(2 * shards + 4),
        out_specs=VMEM_SPEC,
        scratch_shapes=[
            pltpu.VMEM((2 * taps.shape[0] * IDS, length + LANES), bf16),
            pltpu.VMEM((groups, length), f32),
            pltpu.VMEM((channels, length + LANES), bf16),
            pltpu.VMEM((channels, 2 * length + LANES), bf16),
            pltpu.VMEM((channels, length + LANES), f32),
            pltpu.VMEM((channels, span), f32),
        ],
        compiler_params=params(),
        cost_estimate=LARGE_COST,
        name="backward_conv",
    )(me, *slots, *grads, table, taps, skip_gain, mixed)


def run_weight_grad(me, output_grad, hidden, slots):
    shards = len(slots) + 1
    rows, width = output_grad.shape
    share, channels = width // shards, hidden.shape[1]
    return pl.pallas_call(
        functools.partial(weight_grad_kernel, shards),
        out_shape=jax.ShapeDtypeStruct((share, channels), f32),
        in_specs=[SMEM_SPEC, ANY_SPEC] + in_vmem(shards),
        out_specs=VMEM_SPEC,
        scratch_shapes=[pltpu.VMEM((rows, share), bf16), pltpu.SemaphoreType.DMA],
        compiler_params=params(),
        cost_estimate=SMALL_COST,
        name="weight_grad",
    )(me, output_grad, hidden, *slots)


def run_hidden_grad(output_grad, output_weight):
    rows, width = output_grad.shape
    channels = output_weight.shape[1]
    return pl.pallas_call(
        hidden_grad_kernel,
        out_shape=jax.ShapeDtypeStruct((channels, rows), bf16),
        in_specs=[ANY_SPEC, ANY_SPEC],
        out_specs=VMEM_SPEC,
        scratch_shapes=[
            pltpu.VMEM((rows, width), bf16),
            pltpu.VMEM((width, channels), bf16),
            pltpu.VMEM((rows, channels), f32),
            pltpu.SemaphoreType.DMA((2 * CHUNKS,)),
        ],
        compiler_params=params(),
        cost_estimate=SMALL_COST,
        name="hidden_grad",
    )(output_grad, output_weight)


def run_input_grad(core, chips, projection_grad, weight):
    _, rows, channels = projection_grad.shape
    width = weight.shape[1]
    return pl.pallas_call(
        functools.partial(input_grad_kernel, chips),
        out_shape=(
            jax.ShapeDtypeStruct((rows // 2, width), bf16),
            jax.ShapeDtypeStruct((rows // 2, width), bf16),
        ),
        in_specs=[SMEM_SPEC, VMEM_SPEC, ANY_SPEC],
        out_specs=(ANY_SPEC, ANY_SPEC),
        scratch_shapes=[
            pltpu.VMEM(weight.shape, bf16),
            pltpu.VMEM((rows, width // CHUNKS), f32),
            pltpu.VMEM((rows // 2, width), bf16),
            pltpu.VMEM((rows // 2, width), bf16),
            pltpu.SemaphoreType.DMA((CHUNKS,)),
            pltpu.SemaphoreType.DMA((2 * CHUNKS,)),
        ],
        compiler_params=params(),
        cost_estimate=SMALL_COST,
        name="input_grad",
    )(core, projection_grad, weight)


def ctx_exchange(value, step):
    count = lax.axis_size("ctx")
    return lax.ppermute(value, "ctx", [(i, i ^ step) for i in range(count)])


def gather_ctx(value):
    return [value] + [ctx_exchange(value, step) for step in range(1, lax.axis_size("ctx"))]


def tp_exchange(value, mask):
    count = lax.axis_size("tp")
    return lax.ppermute(value, "tp", [(i, i ^ mask) for i in range(count)])


def together(*values):
    return lax.optimization_barrier(values)


def pick(value, index, axis=0):
    return lax.dynamic_index_in_dim(value, index, axis=axis, keepdims=False)


def scalar_array(value):
    return jnp.reshape(value, (1,)).astype(jnp.int32)


def body(
    token_ids,
    embed_table,
    norm_gain,
    input_weight,
    short_weight,
    filters,
    skip_gain,
    output_weight,
    output_grad,
):
    shards = lax.axis_size("ctx")
    chips = lax.axis_size("tp") // 2
    hops = chips - 1
    me = lax.axis_index("ctx")
    core = lax.axis_index("tp") % 2
    chip = lax.axis_index("tp") // 2
    local_rows = token_ids.shape[0]
    width, channels = output_weight.shape
    me_tie, core_tie, chip_tie = scalar_array(me), scalar_array(core), scalar_array(chip)
    weight = jnp.transpose(input_weight, (1, 0, 2))

    groups = filters.shape[0]
    row_number = lax.broadcasted_iota(jnp.int32, (groups + 8, local_rows), 0)
    id_row = jnp.broadcast_to(token_ids[None, :], (groups + 8, local_rows)).astype(f32)
    packed = jnp.where(row_number < groups, jnp.pad(filters, ((0, 8), (0, 0))), id_row)
    slots = gather_ctx(packed)
    hidden_grad = run_hidden_grad(output_grad, output_weight)
    arrived, hidden_grad, me_tie = together(slots[1:], hidden_grad, me_tie)
    slots = [packed] + arrived
    grad_slots = gather_ctx(hidden_grad)

    hidden, mixed, table, for_sibling, mine = run_forward(
        me_tie, core_tie, slots, embed_table, norm_gain, weight, short_weight, skip_gain, output_weight
    )
    for_sibling, mine, hidden, grad_slots = together(for_sibling, mine, hidden, grad_slots)
    half = width // 2
    block_rows = local_rows // chips
    received = tp_exchange(for_sibling, 1)
    mine = mine.reshape(chips, block_rows, half)
    received = received.reshape(chips, block_rows, half)

    order = list(range(2, chips)) + [1]
    share = width // shards

    def out_send(step):
        index = jnp.bitwise_xor(chip, step)
        return (pick(mine, index).astype(f32) + pick(received, index).astype(f32)).astype(bf16)

    def ctx_piece(step):
        start = jnp.bitwise_xor(me, step) * share
        return jnp.concatenate([lax.dynamic_slice_in_dim(output_grad, start, share, axis=1), hidden], axis=1)

    near = range(1, shards // 2 + 1)
    ctx_arrived = [ctx_exchange(ctx_piece(step), step) for step in near]
    sends = [out_send(step) for step in order]
    sends, me_tie = together(sends, me_tie)
    out_arrived = [tp_exchange(value, 2 * step) for step, value in zip(order, sends)]
    projection_grad = run_backward(me_tie, slots, grad_slots, table, short_weight, skip_gain, mixed)
    ctx_sends = [ctx_piece(step) for step in range(shards // 2 + 1, shards)]
    projection_grad, core_tie, ctx_sends = together(projection_grad, core_tie, ctx_sends)
    theirs, mine_grad = run_input_grad(core_tie, chips, projection_grad, weight)
    own_ids = lax.dynamic_slice_in_dim(token_ids, chip * block_rows, block_rows, axis=0)
    own_hot = (own_ids[:, None] == jnp.arange(FIRST_ID, FIRST_ID + IDS)[None, :]).astype(bf16)
    own_letters = lax.dynamic_slice(embed_table, (FIRST_ID, core * half), (IDS, half))
    own_block = jnp.dot(own_hot, own_letters, preferred_element_type=f32)
    own_block = own_block + pick(mine, chip).astype(f32) + pick(received, chip).astype(f32)
    out_arrived, theirs, mine_grad, own_block, ctx_arrived, ctx_sends = together(
        out_arrived, theirs, mine_grad, own_block, ctx_arrived, ctx_sends
    )

    received_grad = tp_exchange(theirs, 1)
    block = own_block
    for value in out_arrived:
        block = block + value.astype(f32)
    block = block.astype(bf16)
    block, received_grad = together(block, received_grad)
    split = (chips, local_rows // (2 * chips), width)
    terms = [mine_grad.reshape(split), received_grad.reshape(split)]

    def pairs(value, which):
        return pick(value.reshape((value.shape[0] // 2, 2) + value.shape[1:]), which, 1)

    def leaving(bit):
        which = 1 - (chip >> bit & 1)
        return sum(pairs(term, which).astype(f32) for term in terms).astype(bf16)

    def keep(bit, arriving):
        which = chip >> bit & 1
        return [pairs(term, which) for term in terms] + [arriving]

    line = [tp_exchange(block, 2 * step) for step in order[:-1]]
    arriving = tp_exchange(leaving(0), 2)
    ctx_more = [
        ctx_exchange(value, step) for step, value in zip(range(shards // 2 + 1, shards), ctx_sends)
    ]
    line, arriving, ctx_more, block = together(line, arriving, ctx_more, block)
    terms = keep(0, arriving)
    levels = chips.bit_length() - 1
    for bit in range(1, levels):
        outgoing = leaving(bit)
        if bit == levels - 1:
            outgoing, block, line, ctx_more = together(outgoing, block, line, ctx_more)
            neighbour = tp_exchange(block, 2)
        terms = keep(bit, tp_exchange(outgoing, 2 << bit))

    line = [block] + line
    base = run_assemble(
        chips, [0] + order[:-1], chip_tie, core_tie, line, [tp_exchange(value, 1) for value in line]
    )
    output_weight_grad = run_weight_grad(me_tie, output_grad, hidden, ctx_arrived + ctx_more)
    kept = sum(term.astype(f32) for term in terms[:-1])
    base, output_weight_grad, neighbour, kept = together(base, output_weight_grad, neighbour, kept)
    block_output = run_insert(chip_tie, core_tie, neighbour, tp_exchange(neighbour, 1), base)
    normed_grad = (kept + terms[-1].astype(f32)).reshape(local_rows // (2 * chips), width)
    return (block_output, output_weight_grad, jnp.transpose(projection_grad, (1, 0, 2)), normed_grad)


def solution(mesh):
    in_specs = (
        P("ctx"),
        P(),
        P(),
        P(None, None, "tp"),
        P(None, None, "tp"),
        P("tp", "ctx"),
        P("tp"),
        P(None, "tp"),
        P("ctx", None),
    )
    out_specs = (P("ctx", None), P("ctx", "tp"), P("ctx", None, "tp"), P(("ctx", "tp"), None))
    return jax.shard_map(body, mesh=mesh, in_specs=in_specs, out_specs=out_specs, check_vma=False)
```

```python
import functools

import jax
import jax.numpy as jnp
from jax import lax
from jax.experimental import pallas as pl
from jax.experimental.pallas import tpu as pltpu
from jax.sharding import PartitionSpec as P

LANES = 128
FIRST_ID = 64
IDS = 32
VMEM_BYTES = 56 * 1024 * 1024
f32 = jnp.float32
bf16 = jnp.bfloat16
CONTRACT_LAST = (((1,), (1,)), ((), ()))


def one_hot(ids, taps):
    length = ids.shape[1]
    lane = lax.broadcasted_iota(jnp.int32, (1, length), 1)
    code = lax.broadcasted_iota(jnp.int32, (IDS, length), 0) + FIRST_ID
    rows = []
    for tap in range(taps):
        moved = ids if tap == 0 else jnp.where(lane < tap, 0, pltpu.roll(ids, tap, axis=1))
        rows.append(jnp.where(code == moved, 1.0, 0.0))
    return jnp.concatenate(rows, axis=0)


def tap_weights(taps_ref, table_ref, part):
    table = table_ref[part]
    value = jnp.concatenate([taps_ref[i, part][None, :] * table for i in range(taps_ref.shape[0])], axis=0)
    high = value.astype(bf16).astype(f32)
    return jnp.concatenate([high, value - high], axis=0).astype(bf16)


def expand(weights, hot):
    return lax.dot_general(weights, hot, (((0,), (0,)), ((), ())), preferred_element_type=f32)


def toeplitz_tiles(row, blocks, mirrored):
    sub = lax.broadcasted_iota(jnp.int32, (LANES, LANES), 0)
    lane = lax.broadcasted_iota(jnp.int32, (LANES, LANES), 1)
    keep = lane <= sub if mirrored else lane >= sub
    before = jnp.zeros((LANES, LANES), f32)
    tiles = []
    for q in range(blocks):
        part = jnp.broadcast_to(row[:, LANES * q : LANES * (q + 1)], (LANES, LANES))
        turned = pltpu.roll(part, 1 if mirrored else 0, 1, stride=1, stride_axis=0)
        tiles.append(jnp.where(keep, turned, before).astype(bf16))
        before = turned
    return tiles


def reverse_blocks(value):
    sub = lax.broadcasted_iota(jnp.int32, (LANES, LANES), 0)
    lane = lax.broadcasted_iota(jnp.int32, (LANES, LANES), 1)
    mirror = jnp.where(sub + lane == LANES - 1, 1.0, 0.0).astype(bf16)
    blocks = [value[:, start : start + LANES].astype(bf16) for start in range(0, value.shape[1], LANES)]
    return jnp.concatenate([jnp.dot(block, mirror, preferred_element_type=f32) for block in blocks], axis=1)


def lanes_at(block, count):
    return pl.ds(pl.multiple_of(block * LANES, LANES), count * LANES)


def channel_columns(taps_ref, skip_ref):
    taps = taps_ref.shape[0]
    rows = [taps_ref[i] for i in range(taps)] + [skip_ref[...][None, :]]
    channels = skip_ref.shape[0]
    rows.append(jnp.zeros((LANES - 3 * taps - 1, channels), f32))
    return jnp.transpose(jnp.concatenate(rows, axis=0))


def place_slots(me, local_blocks, slots, store):
    for step, slot in enumerate(slots):
        store(lanes_at(jnp.bitwise_xor(me, step) * local_blocks, local_blocks), slot)


def start_rows(source_ref, start, held, arrived):
    copies = []
    chunk = held.shape[0] // arrived.shape[0]
    for index in range(arrived.shape[0]):
        rows = pl.ds(pl.multiple_of(start + index * chunk, chunk), chunk)
        copies.append(
            pltpu.make_async_copy(source_ref.at[rows], held.at[index * chunk : (index + 1) * chunk], arrived.at[index])
        )
        copies[-1].start()
    return copies


def split_blocks(total, chip, rows, send, kept, columns):
    for index in range(total.shape[0] // (2 * rows)):
        place = slice(index * rows, (index + 1) * rows)
        for target, bit in ((send, 1 - chip % 2), (kept, chip % 2)):
            source = pl.ds(pl.multiple_of((2 * index + bit) * rows, 8), rows)
            target[place, columns] = total[source].astype(target.dtype)


def write_out(pairs, columns, left, first):
    copies = []
    for index, (source, target) in enumerate(pairs):
        copies.append(pltpu.make_async_copy(source.at[:, columns], target.at[:, columns], left.at[first + index]))
        copies[-1].start()
    return copies


def project_kernel(
    chips, core_ref, chip_ref, hidden_ref, other_ref, weight_ref, other_weight_ref, ids_ref, letters_ref,
    send_ref, kept_ref, weight, arrived, other_weight, other_arrived, total, send, kept, left, letters, letters_arrived,
):
    half = weight.shape[0]
    start = core_ref[0] * half
    copies = start_rows(weight_ref, start, weight, arrived)
    other_copies = start_rows(other_weight_ref, start, other_weight, other_arrived)
    own_columns = pl.ds(pl.multiple_of(start, half), half)
    letters_copy = pltpu.make_async_copy(letters_ref.at[FIRST_ID : FIRST_ID + IDS, own_columns], letters, letters_arrived)
    letters_copy.start()
    rows = total.shape[0] // chips
    lane = lax.broadcasted_iota(jnp.int32, (IDS, total.shape[0]), 1)
    first = chip_ref[0] * rows
    marks = one_hot(ids_ref[ids_ref.shape[0] - 8 : ids_ref.shape[0] - 7].astype(jnp.int32), 1)
    marks = jnp.where(jnp.logical_and(lane >= first, lane < first + rows), marks, 0.0).astype(bf16)
    letters_copy.wait()
    chunk = half // len(copies)
    hidden, other = hidden_ref[...], other_ref[...]
    leaving = []
    for index in range(len(copies)):
        columns = slice(index * chunk, (index + 1) * chunk)
        copies[index].wait()
        other_copies[index].wait()
        total[...] = (
            lax.dot_general(hidden, weight[columns], CONTRACT_LAST, preferred_element_type=f32)
            + lax.dot_general(other, other_weight[columns], CONTRACT_LAST, preferred_element_type=f32)
            + expand(marks, letters[:, columns])
        )
        split_blocks(total, chip_ref[0], rows, send, kept, columns)
        leaving += write_out(((send, send_ref), (kept, kept_ref)), columns, left, 2 * index)
    for copy in leaving:
        copy.wait()


def assemble_kernel(rows, steps, chip_ref, core_ref, *refs):
    out_ref = refs[-1]
    columns = refs[0].shape[1]
    for index, held in enumerate(steps + steps):
        side = core_ref[0] if index < len(steps) else 1 - core_ref[0]
        for slot, step in enumerate(held):
            place = pl.ds(pl.multiple_of(jnp.bitwise_xor(chip_ref[0], step) * rows, rows), rows)
            at = (place, pl.ds(pl.multiple_of(side * columns, columns), columns))
            out_ref[at] = refs[index][slot * rows : (slot + 1) * rows]


def forward_kernel(shards, me_ref, *refs):
    slots = refs[:shards]
    letters_ref, gain_ref, weight_ref, taps_ref, skip_ref = refs[shards : shards + 5]
    hidden_ref, mixed_ref, table_ref = refs[shards + 5 : shards + 8]
    normed, hot, filters, matrices, signal, exact, long_part, weight, arrived, table, left = refs[shards + 8 :]
    groups = filters.shape[0]
    local_rows = slots[0].shape[1]
    channels = table.shape[2]
    width = channels // groups
    local_blocks = local_rows // LANES
    blocks = shards * local_blocks
    length = blocks * LANES
    window = local_blocks + 1
    chunks = arrived.shape[0]
    chunk = weight.shape[1] // chunks
    taps = taps_ref.shape[0]
    me = me_ref[0]
    first = me * local_blocks

    copies = []
    for index in range(chunks):
        rows = slice(index * chunk, (index + 1) * chunk)
        copies.append(pltpu.make_async_copy(weight_ref.at[:, rows], weight.at[:, rows], arrived.at[index]))
        copies[-1].start()
    for index, slot in enumerate(slots):
        place = lanes_at(jnp.bitwise_xor(me, index) * local_blocks, local_blocks)
        filters[:, place] = slot[:groups]
        exact[0:1, place] = slot[groups : groups + 1]
    marks = one_hot(exact[0:1, :length].astype(jnp.int32), taps)
    hot[:, :length] = jnp.concatenate([marks, marks], axis=0).astype(bf16)
    hot[:, length:] = jnp.zeros((hot.shape[0], LANES), bf16)
    signal[:, :length] = jnp.zeros((channels, length), bf16)
    signal[:, 2 * length :] = jnp.zeros((channels, LANES), bf16)
    exact[:, length:] = jnp.zeros((channels, LANES), f32)
    values = letters_ref[...].astype(f32)
    inverse = lax.rsqrt(jnp.mean(values * values, axis=-1, keepdims=True) + 1e-06)
    normed[...] = (values * inverse * gain_ref[...][None, :]).astype(bf16)

    def one_matrix(group, carry):
        tiles = toeplitz_tiles(filters[pl.ds(group, 1), :], blocks, False)
        for q in range(blocks):
            matrices[group, (blocks - 1 - q) * LANES : (blocks - q) * LANES] = tiles[q]
        return carry

    for index in range(chunks):
        lax.fori_loop(index * groups // chunks, (index + 1) * groups // chunks, one_matrix, 0)
        rows = slice(index * chunk, (index + 1) * chunk)
        copies[index].wait()
        for part in range(3):
            term = jnp.dot(normed[:, rows], weight[part, rows], preferred_element_type=f32)
            table[part] = term if index == 0 else table[part] + term

    table_copy = pltpu.make_async_copy(table, table_ref, left.at[0])
    table_copy.start()
    key_weights = tap_weights(taps_ref, table, 1)
    value_weights = tap_weights(taps_ref, table, 2)
    for start in range(0, channels, LANES):
        rows = slice(start, start + LANES)
        mixture = expand(key_weights[:, rows], hot[:, :length]) * expand(value_weights[:, rows], hot[:, :length])
        exact[rows, :length] = mixture
        signal[rows, length : 2 * length] = mixture.astype(bf16)

    def one_group(group, carry):
        rows = pl.ds(pl.multiple_of(group * width, width), width)
        left = jnp.concatenate([signal[rows, lanes_at(first + i + 1, blocks)] for i in range(window)], axis=0)
        result = jnp.dot(left, matrices[group], preferred_element_type=f32)
        for i in range(window):
            long_part[rows, i * LANES : (i + 1) * LANES] = result[i * width : (i + 1) * width]
        return carry

    lax.fori_loop(0, groups, one_group, 0, unroll=4)
    columns = channel_columns(taps_ref, skip_ref)
    mixed = columns[:, 3 * taps : 3 * taps + 1] * exact[:, lanes_at(first, window)] + long_part[...]
    long_part[...] = mixed
    mixed_copy = pltpu.make_async_copy(long_part, mixed_ref, left.at[1])
    mixed_copy.start()
    queries = expand(tap_weights(taps_ref, table, 0), hot[:, lanes_at(first, local_blocks)])
    hidden_ref[...] = jnp.transpose(queries * mixed[:, :local_rows]).astype(bf16)
    table_copy.wait()
    mixed_copy.wait()


def backward_kernel(shards, me_ref, *refs):
    slots, grad_slots = refs[:shards], refs[shards : 2 * shards]
    table_ref, taps_ref, skip_ref, mixed_ref, out_ref = refs[2 * shards : 2 * shards + 5]
    hot, filters, grads, signal, exact, long_part = refs[2 * shards + 5 :]
    me = me_ref[0]
    groups = filters.shape[0]
    local_rows = slots[0].shape[1]
    channels = table_ref.shape[2]
    width = channels // groups
    local_blocks = local_rows // LANES
    blocks = shards * local_blocks
    length = blocks * LANES
    window = local_blocks + 1
    taps = taps_ref.shape[0]

    for step in range(shards):
        place = lanes_at(jnp.bitwise_xor(me, step) * local_blocks, local_blocks)
        exact[0:1, place] = slots[step][groups : groups + 1]
        filters[:, place] = reverse_blocks(slots[step][:groups])
        grads[:, place] = grad_slots[step][...]
    grads[:, length:] = jnp.zeros((channels, LANES), bf16)
    marks = one_hot(exact[0:1, :length].astype(jnp.int32), taps)
    hot[:, :length] = jnp.concatenate([marks, marks], axis=0).astype(bf16)
    hot[:, length:] = jnp.zeros((hot.shape[0], LANES), bf16)

    signal[:, length:] = jnp.zeros((channels, length + LANES), bf16)
    exact[:, length:] = jnp.zeros((channels, LANES), f32)
    query_weights = tap_weights(taps_ref, table_ref, 0)
    for start in range(0, channels, LANES):
        rows = slice(start, start + LANES)
        mixed_grad = expand(query_weights[:, rows], hot[:, :length]) * grads[rows, :length].astype(f32)
        exact[rows, :length] = mixed_grad
        signal[rows, :length] = mixed_grad.astype(bf16)

    first = me * local_blocks

    def one_group(group, carry):
        matrix = jnp.concatenate(toeplitz_tiles(filters[pl.ds(group, 1), :], blocks, True), axis=0)
        rows = pl.ds(pl.multiple_of(group * width, width), width)
        left = jnp.concatenate([signal[rows, lanes_at(first + i, blocks)] for i in range(window)], axis=0)
        result = jnp.dot(left, matrix, preferred_element_type=f32)
        for i in range(window):
            long_part[rows, i * LANES : (i + 1) * LANES] = result[i * width : (i + 1) * width]
        return carry

    lax.fori_loop(0, groups, one_group, 0, unroll=4)
    own = lanes_at(first, window)
    columns = channel_columns(taps_ref, skip_ref)
    mixture_grad = columns[:, 3 * taps : 3 * taps + 1] * exact[:, own] + long_part[...]
    span = window * LANES
    for part in range(3):
        if part == 0:
            feature_grad = grads[:, own].astype(f32) * mixed_ref[...]
        else:
            other = expand(tap_weights(taps_ref, table_ref, 3 - part), hot[:, own])
            feature_grad = mixture_grad * other
        total = columns[:, part : part + 1] * feature_grad
        for tap in range(1, taps):
            column = 3 * tap + part
            total = total + columns[:, column : column + 1] * pltpu.roll(feature_grad, span - tap, axis=1)
        out_ref[part] = jnp.transpose(total[:, :local_rows]).astype(bf16)


def hidden_grad_kernel(grad_ref, weight_ref, out_ref, grad, weight, total, arrived):
    chunks = arrived.shape[0] // 2
    chunk = weight.shape[0] // chunks
    copies = []
    for index in range(chunks):
        part = slice(index * chunk, (index + 1) * chunk)
        copies.append(pltpu.make_async_copy(grad_ref.at[:, part], grad.at[:, part], arrived.at[2 * index]))
        copies.append(pltpu.make_async_copy(weight_ref.at[part], weight.at[part], arrived.at[2 * index + 1]))
    for copy in copies:
        copy.start()
    for index in range(chunks):
        part = slice(index * chunk, (index + 1) * chunk)
        copies[2 * index].wait()
        copies[2 * index + 1].wait()
        term = jnp.dot(grad[:, part], weight[part], preferred_element_type=f32)
        total[...] = term if index == 0 else total[...] + term
    out_ref[...] = jnp.transpose(total[...]).astype(bf16)


def input_grad_kernel(
    chips, core_ref, chip_ref, grad_ref, other_grad_ref, weight_ref, other_weight_ref,
    send_ref, kept_ref, weight, other_weight, arrived, total, send, kept, left,
):
    half = weight.shape[1]
    chunks = arrived.shape[0] // 2
    chunk = half // chunks
    copies = []
    for index in range(chunks):
        columns = slice(index * chunk, (index + 1) * chunk)
        source = pl.ds(pl.multiple_of(core_ref[0] * half + index * chunk, chunk), chunk)
        pair = (
            pltpu.make_async_copy(weight_ref.at[:, source], weight.at[:, columns], arrived.at[2 * index]),
            pltpu.make_async_copy(other_weight_ref.at[:, source], other_weight.at[:, columns], arrived.at[2 * index + 1]),
        )
        for copy in pair:
            copy.start()
        copies.append(pair)
    rows = total.shape[0] // chips
    leaving = []
    for index in range(chunks):
        columns = slice(index * chunk, (index + 1) * chunk)
        value = None
        for copy, grad, held in zip(copies[index], (grad_ref, other_grad_ref), (weight, other_weight)):
            copy.wait()
            for part in range(3):
                term = lax.dot_general(grad[part], held[part, columns], CONTRACT_LAST, preferred_element_type=f32)
                value = term if value is None else value + term
        total[...] = value
        split_blocks(total, chip_ref[0], rows, send, kept, columns)
        leaving += write_out(((send, send_ref), (kept, kept_ref)), columns, left, 2 * index)
    for copy in leaving:
        copy.wait()


def weight_grad_kernel(shards, me_ref, core_ref, grad_ref, *refs):
    hidden, mine, theirs = refs[:shards], refs[shards : 2 * shards - 1], refs[2 * shards - 1 : 3 * shards - 2]
    out_ref, own, arrived = refs[3 * shards - 2 :]
    share = own.shape[1]
    part = share // 2
    source = grad_ref.at[:, pl.ds(pl.multiple_of(me_ref[0] * share, share), share)]
    copy = pltpu.make_async_copy(source, own, arrived)
    copy.start()
    for slots, side in ((mine, core_ref[0]), (theirs, 1 - core_ref[0])):
        total = None
        for slot, shard_hidden in zip(slots, hidden[1:]):
            term = expand(slot[...], shard_hidden[...])
            total = term if total is None else total + term
        if slots is mine:
            copy.wait()
        place = pl.ds(pl.multiple_of(side * part, part), part)
        out_ref[place, :] = total + expand(own[:, place], hidden[0][...])


def in_vmem(count):
    return [pl.BlockSpec(memory_space=pltpu.VMEM)] * count


SMEM_SPEC = pl.BlockSpec(memory_space=pltpu.SMEM)
ANY_SPEC = pl.BlockSpec(memory_space=pl.ANY)
VMEM_SPEC = pl.BlockSpec(memory_space=pltpu.VMEM)
CHUNKS = 8


def params():
    return pltpu.CompilerParams(vmem_limit_bytes=VMEM_BYTES)


LARGE_COST = pl.CostEstimate(flops=20_000_000_000, bytes_accessed=10_000_000, transcendentals=0)
SMALL_COST = pl.CostEstimate(flops=1000, bytes_accessed=1000, transcendentals=0)


def insert_kernel(rows, steps, chip_ref, core_ref, own_ref, theirs_ref, base_ref, out_ref, moved):
    columns = own_ref.shape[1]
    copies = []
    for index, step in enumerate(steps):
        place = pl.ds(pl.multiple_of(jnp.bitwise_xor(chip_ref[0], step) * rows, rows), rows)
        for which, source in enumerate((own_ref, theirs_ref)):
            side = core_ref[0] if which == 0 else 1 - core_ref[0]
            target = out_ref.at[place, pl.ds(pl.multiple_of(side * columns, columns), columns)]
            part = source.at[index * rows : (index + 1) * rows]
            copies.append(pltpu.make_async_copy(part, target, moved.at[2 * index + which]))
            copies[-1].start()
    for copy in copies:
        copy.wait()


def run_insert(steps, chip, core, own, theirs, base):
    return pl.pallas_call(
        functools.partial(insert_kernel, own.shape[0] // len(steps), steps),
        out_shape=jax.ShapeDtypeStruct(base.shape, base.dtype),
        in_specs=[SMEM_SPEC, SMEM_SPEC, VMEM_SPEC, VMEM_SPEC, ANY_SPEC],
        out_specs=ANY_SPEC,
        scratch_shapes=[pltpu.SemaphoreType.DMA((2 * len(steps),))],
        input_output_aliases={4: 0},
        compiler_params=params(),
        cost_estimate=SMALL_COST,
        name="insert",
    )(chip, core, own, theirs, base)


def run_assemble(chips, steps, chip, core, own, theirs):
    rows, columns = own[0].shape
    return pl.pallas_call(
        functools.partial(assemble_kernel, rows, steps),
        out_shape=jax.ShapeDtypeStruct((chips * rows, 2 * columns), bf16),
        in_specs=[SMEM_SPEC, SMEM_SPEC] + in_vmem(2 * len(own)),
        out_specs=VMEM_SPEC,
        compiler_params=params(),
        cost_estimate=SMALL_COST,
        name="assemble",
    )(chip, core, *own, *theirs)


def run_forward(me, slots, embed_table, norm_gain, weight, taps, skip_gain):
    shards = len(slots)
    local_rows = slots[0].shape[1]
    _, width, channels = weight.shape
    groups = slots[0].shape[0] - 8
    length = shards * local_rows
    span = local_rows + LANES
    return pl.pallas_call(
        functools.partial(forward_kernel, shards),
        grid=(1,),
        out_shape=(
            jax.ShapeDtypeStruct((local_rows, channels), bf16),
            jax.ShapeDtypeStruct((channels, span), f32),
            jax.ShapeDtypeStruct((3, IDS, channels), f32),
        ),
        in_specs=[SMEM_SPEC]
        + in_vmem(shards)
        + [pl.BlockSpec((IDS, width), lambda step: (FIRST_ID // IDS, 0)), VMEM_SPEC, ANY_SPEC, VMEM_SPEC, VMEM_SPEC],
        out_specs=(VMEM_SPEC, ANY_SPEC, ANY_SPEC),
        scratch_shapes=[
            pltpu.VMEM((IDS, width), bf16),
            pltpu.VMEM((2 * taps.shape[0] * IDS, length + LANES), bf16),
            pltpu.VMEM((groups, length), f32),
            pltpu.VMEM((groups, length, LANES), bf16),
            pltpu.VMEM((channels, 2 * length + LANES), bf16),
            pltpu.VMEM((channels, length + LANES), f32),
            pltpu.VMEM((channels, span), f32),
            pltpu.VMEM(weight.shape, bf16),
            pltpu.SemaphoreType.DMA((CHUNKS,)),
            pltpu.VMEM((3, IDS, channels), f32),
            pltpu.SemaphoreType.DMA((2,)),
        ],
        compiler_params=params(),
        cost_estimate=LARGE_COST,
        name="forward_conv",
    )(me, *slots, embed_table, norm_gain, weight, taps, skip_gain)


def run_project(core, chip, chips, hidden, other_hidden, weight, other_weight, packed, embed_table):
    rows, channels = hidden.shape
    half = weight.shape[0] // 2
    return pl.pallas_call(
        functools.partial(project_kernel, chips),
        out_shape=(jax.ShapeDtypeStruct((rows // 2, half), bf16), jax.ShapeDtypeStruct((rows // 2, half), f32)),
        in_specs=[SMEM_SPEC, SMEM_SPEC, VMEM_SPEC, VMEM_SPEC, ANY_SPEC, ANY_SPEC, VMEM_SPEC, ANY_SPEC],
        out_specs=(ANY_SPEC, ANY_SPEC),
        scratch_shapes=[
            pltpu.VMEM((half, channels), bf16),
            pltpu.SemaphoreType.DMA((4,)),
            pltpu.VMEM((half, channels), bf16),
            pltpu.SemaphoreType.DMA((4,)),
            pltpu.VMEM((rows, half // 4), f32),
            pltpu.VMEM((rows // 2, half), bf16),
            pltpu.VMEM((rows // 2, half), f32),
            pltpu.SemaphoreType.DMA((8,)),
            pltpu.VMEM((IDS, half), bf16),
            pltpu.SemaphoreType.DMA,
        ],
        compiler_params=params(),
        cost_estimate=SMALL_COST,
        name="project",
    )(core, chip, hidden, other_hidden, weight, other_weight, packed, embed_table)


def run_backward(me, slots, grads, table, taps, skip_gain, mixed):
    shards = len(slots)
    local_rows = slots[0].shape[1]
    channels = table.shape[2]
    groups = slots[0].shape[0] - 8
    length = shards * local_rows
    span = local_rows + LANES
    return pl.pallas_call(
        functools.partial(backward_kernel, shards),
        out_shape=jax.ShapeDtypeStruct((3, local_rows, channels), bf16),
        in_specs=[SMEM_SPEC] + in_vmem(2 * shards + 4),
        out_specs=VMEM_SPEC,
        scratch_shapes=[
            pltpu.VMEM((2 * taps.shape[0] * IDS, length + LANES), bf16),
            pltpu.VMEM((groups, length), f32),
            pltpu.VMEM((channels, length + LANES), bf16),
            pltpu.VMEM((channels, 2 * length + LANES), bf16),
            pltpu.VMEM((channels, length + LANES), f32),
            pltpu.VMEM((channels, span), f32),
        ],
        compiler_params=params(),
        cost_estimate=LARGE_COST,
        name="backward_conv",
    )(me, *slots, *grads, table, taps, skip_gain, mixed)


def run_weight_grad(me, core, output_grad, hidden, mine, theirs):
    shards = len(hidden)
    rows, width = output_grad.shape
    share, channels = width // shards, hidden[0].shape[1]
    return pl.pallas_call(
        functools.partial(weight_grad_kernel, shards),
        out_shape=jax.ShapeDtypeStruct((share, channels), f32),
        in_specs=[SMEM_SPEC, SMEM_SPEC, ANY_SPEC] + in_vmem(3 * shards - 2),
        out_specs=VMEM_SPEC,
        scratch_shapes=[pltpu.VMEM((rows, share), bf16), pltpu.SemaphoreType.DMA],
        compiler_params=params(),
        cost_estimate=SMALL_COST,
        name="weight_grad",
    )(me, core, output_grad, *hidden, *mine, *theirs)


def run_hidden_grad(output_grad, output_weight):
    rows, width = output_grad.shape
    channels = output_weight.shape[1]
    return pl.pallas_call(
        hidden_grad_kernel,
        out_shape=jax.ShapeDtypeStruct((channels, rows), bf16),
        in_specs=[ANY_SPEC, ANY_SPEC],
        out_specs=VMEM_SPEC,
        scratch_shapes=[
            pltpu.VMEM((rows, width), bf16),
            pltpu.VMEM((width, channels), bf16),
            pltpu.VMEM((rows, channels), f32),
            pltpu.SemaphoreType.DMA((2 * CHUNKS,)),
        ],
        compiler_params=params(),
        cost_estimate=SMALL_COST,
        name="hidden_grad",
    )(output_grad, output_weight)


def run_input_grad(core, chip, chips, grad, other_grad, weight, other_weight):
    _, rows, channels = grad.shape
    half = weight.shape[1] // 2
    return pl.pallas_call(
        functools.partial(input_grad_kernel, chips),
        out_shape=(jax.ShapeDtypeStruct((rows // 2, half), bf16), jax.ShapeDtypeStruct((rows // 2, half), f32)),
        in_specs=[SMEM_SPEC, SMEM_SPEC, VMEM_SPEC, VMEM_SPEC, ANY_SPEC, ANY_SPEC],
        out_specs=(ANY_SPEC, ANY_SPEC),
        scratch_shapes=[
            pltpu.VMEM((3, half, channels), bf16),
            pltpu.VMEM((3, half, channels), bf16),
            pltpu.SemaphoreType.DMA((8,)),
            pltpu.VMEM((rows, half // 4), f32),
            pltpu.VMEM((rows // 2, half), bf16),
            pltpu.VMEM((rows // 2, half), f32),
            pltpu.SemaphoreType.DMA((8,)),
        ],
        compiler_params=params(),
        cost_estimate=SMALL_COST,
        name="input_grad",
    )(core, chip, grad, other_grad, weight, other_weight)


def ctx_exchange(value, step):
    count = lax.axis_size("ctx")
    return lax.ppermute(value, "ctx", [(i, i ^ step) for i in range(count)])


def gather_ctx(value):
    return [value] + [ctx_exchange(value, step) for step in range(1, lax.axis_size("ctx"))]


def tp_exchange(value, mask):
    count = lax.axis_size("tp")
    return lax.ppermute(value, "tp", [(i, i ^ mask) for i in range(count)])


def together(*values):
    return lax.optimization_barrier(values)


def pick(value, index, axis=0):
    return lax.dynamic_index_in_dim(value, index, axis=axis, keepdims=False)


def scalar_array(value):
    return jnp.reshape(value, (1,)).astype(jnp.int32)


def body(
    token_ids,
    embed_table,
    norm_gain,
    input_weight,
    short_weight,
    filters,
    skip_gain,
    output_weight,
    output_grad,
):
    shards = lax.axis_size("ctx")
    chips = lax.axis_size("tp") // 2
    hops = chips - 1
    me = lax.axis_index("ctx")
    core = lax.axis_index("tp") % 2
    chip = lax.axis_index("tp") // 2
    local_rows = token_ids.shape[0]
    width, channels = output_weight.shape
    me_tie, core_tie, chip_tie = scalar_array(me), scalar_array(core), scalar_array(chip)
    weight = jnp.transpose(input_weight, (1, 0, 2))

    groups = filters.shape[0]
    row_number = lax.broadcasted_iota(jnp.int32, (groups + 8, local_rows), 0)
    id_row = jnp.broadcast_to(token_ids[None, :], (groups + 8, local_rows)).astype(f32)
    packed = jnp.where(row_number < groups, jnp.pad(filters, ((0, 8), (0, 0))), id_row)
    slots = gather_ctx(packed)
    half = width // 2
    levels = chips.bit_length() - 1
    block_rows = local_rows // chips
    other_weight, other_input = tp_exchange(output_weight, 1), tp_exchange(weight, 1)
    hidden_grad = run_hidden_grad(output_grad, output_weight)
    arrived, hidden_grad, me_tie = together(slots[1:], hidden_grad, me_tie)
    slots = [packed] + arrived
    grad_slots = gather_ctx(hidden_grad)

    hidden, mixed, table = run_forward(
        me_tie, slots, embed_table, norm_gain, weight, short_weight, skip_gain
    )
    hidden, grad_slots, other_weight = together(hidden, grad_slots, other_weight)
    send, kept = run_project(
        core_tie, chip_tie, chips, hidden, tp_exchange(hidden, 1), output_weight, other_weight, packed, embed_table
    )

    def pairs(value, which):
        return pick(value.reshape((value.shape[0] // 2, 2) + value.shape[1:]), which, 1)

    def leaving(terms, bit):
        which = 1 - (chip >> bit & 1)
        return sum(pairs(term, which).astype(f32) for term in terms).astype(bf16)

    def keep(terms, bit):
        which = chip >> bit & 1
        return [pairs(term, which) for term in terms]

    blocks = (chips // 2, block_rows, half)
    send, kept, me_tie, late_hidden = together(send, kept, me_tie, hidden)
    out_arrived = tp_exchange(send, 2)

    share = width // shards
    part = share // 2

    def ctx_piece(step):
        start = jnp.bitwise_xor(me, step) * share + core * part
        return lax.dynamic_slice_in_dim(output_grad, start, part, axis=1)

    near, others = range(1, shards // 2 + 1), range(shards // 2 + 1, shards)
    pieces = [ctx_piece(step) for step in range(1, shards)]
    pieces, me_tie = together(pieces, me_tie)
    near_grad = [ctx_exchange(pieces[step - 1], step) for step in near]
    projection_grad = run_backward(me_tie, slots, grad_slots, table, short_weight, skip_gain, mixed)
    projection_grad, near_grad, late_hidden = together(projection_grad, near_grad, late_hidden)
    other_grad = tp_exchange(projection_grad, 1)
    near_hidden = [ctx_exchange(late_hidden, step) for step in near]
    grad_send, grad_kept = run_input_grad(
        core_tie, chip_tie, chips, projection_grad, other_grad, weight, other_input
    )
    out_terms = [kept.reshape(blocks), out_arrived.reshape(blocks)]
    for bit in range(1, levels):
        out_terms = keep(out_terms, bit) + [tp_exchange(leaving(out_terms, bit), 2 << bit)]
    grad_send, grad_kept, near_hidden, late_hidden, pieces = together(
        grad_send, grad_kept, near_hidden, late_hidden, pieces
    )
    grad_arrived = tp_exchange(grad_send, 2)
    far_grad = [ctx_exchange(pieces[step - 1], step) for step in others]
    far_hidden = [ctx_exchange(late_hidden, step) for step in others]

    block = sum(term.astype(f32) for term in out_terms).reshape(block_rows, half).astype(bf16)
    line, steps = [block], [[0]]
    for level in range(levels - 1):
        mask = chips >> level + 1
        held = line[0] if level == 0 else jnp.concatenate(line, axis=0)
        line.append(tp_exchange(held, 2 * mask))
        steps.append([step ^ mask for group in steps for step in group])
    grad_arrived, far_grad, far_hidden = together(grad_arrived, far_grad, far_hidden)
    grad_terms = [grad_kept.reshape(blocks), grad_arrived.reshape(blocks)]
    for bit in range(1, levels):
        grad_terms = keep(grad_terms, bit) + [tp_exchange(leaving(grad_terms, bit), 2 << bit)]
    came = tp_exchange(jnp.concatenate(line, axis=0), 2)
    came_steps = [step ^ 1 for group in steps for step in group]

    base = run_assemble(chips, steps, chip_tie, core_tie, line, [tp_exchange(value, 1) for value in line])
    mine = near_grad + far_grad
    output_weight_grad = run_weight_grad(
        me_tie, core_tie, output_grad, [late_hidden] + near_hidden + far_hidden, mine,
        [tp_exchange(value, 1) for value in mine],
    )
    kept_sum = sum(term.astype(f32) for term in grad_terms[:-1])
    base, output_weight_grad, came, kept_sum, last = together(
        base, output_weight_grad, came, kept_sum, grad_terms[-1]
    )
    total = (kept_sum + last.astype(f32)).reshape(2, block_rows // 2, half)
    my_rows, their_rows = pick(total, core), pick(total, 1 - core)
    other_columns = tp_exchange(their_rows, 1)
    block_output = run_insert(came_steps, chip_tie, core_tie, came, tp_exchange(came, 1), base)
    normed_grad = jnp.where(
        core == 0,
        jnp.concatenate([my_rows, other_columns], axis=1),
        jnp.concatenate([other_columns, my_rows], axis=1),
    )
    return (block_output, output_weight_grad, jnp.transpose(projection_grad, (1, 0, 2)), normed_grad)


def solution(mesh):
    in_specs = (
        P("ctx"),
        P(),
        P(),
        P(None, None, "tp"),
        P(None, None, "tp"),
        P("tp", "ctx"),
        P("tp"),
        P(None, "tp"),
        P("ctx", None),
    )
    out_specs = (P("ctx", None), P("ctx", "tp"), P("ctx", None, "tp"), P(("ctx", "tp"), None))
    return jax.shard_map(body, mesh=mesh, in_specs=in_specs, out_specs=out_specs, check_vma=False)
```

```python
import functools

import jax
import jax.numpy as jnp
from jax import lax
from jax.experimental import pallas as pl
from jax.experimental.pallas import tpu as pltpu
from jax.sharding import PartitionSpec as P

LANES = 128
FIRST_ID = 64
IDS = 32
VMEM_BYTES = 56 * 1024 * 1024
f32 = jnp.float32
bf16 = jnp.bfloat16
CONTRACT_LAST = (((1,), (1,)), ((), ()))


def one_hot(ids, taps):
    length = ids.shape[1]
    lane = lax.broadcasted_iota(jnp.int32, (1, length), 1)
    code = lax.broadcasted_iota(jnp.int32, (IDS, length), 0) + FIRST_ID
    rows = []
    for tap in range(taps):
        moved = ids if tap == 0 else jnp.where(lane < tap, 0, pltpu.roll(ids, tap, axis=1))
        rows.append(jnp.where(code == moved, 1.0, 0.0))
    return jnp.concatenate(rows, axis=0)


def tap_weights(taps_ref, table_ref, part):
    table = table_ref[part]
    value = jnp.concatenate([taps_ref[i, part][None, :] * table for i in range(taps_ref.shape[0])], axis=0)
    high = value.astype(bf16).astype(f32)
    return jnp.concatenate([high, value - high], axis=0).astype(bf16)


def expand(weights, hot):
    return lax.dot_general(weights, hot, (((0,), (0,)), ((), ())), preferred_element_type=f32)


def toeplitz_tiles(row, blocks, mirrored):
    sub = lax.broadcasted_iota(jnp.int32, (LANES, LANES), 0)
    lane = lax.broadcasted_iota(jnp.int32, (LANES, LANES), 1)
    keep = lane <= sub if mirrored else lane >= sub
    before = jnp.zeros((LANES, LANES), f32)
    tiles = []
    for q in range(blocks):
        part = jnp.broadcast_to(row[:, LANES * q : LANES * (q + 1)], (LANES, LANES))
        turned = pltpu.roll(part, 1 if mirrored else 0, 1, stride=1, stride_axis=0)
        tiles.append(jnp.where(keep, turned, before).astype(bf16))
        before = turned
    return tiles


def reverse_blocks(value):
    sub = lax.broadcasted_iota(jnp.int32, (LANES, LANES), 0)
    lane = lax.broadcasted_iota(jnp.int32, (LANES, LANES), 1)
    mirror = jnp.where(sub + lane == LANES - 1, 1.0, 0.0).astype(bf16)
    blocks = [value[:, start : start + LANES].astype(bf16) for start in range(0, value.shape[1], LANES)]
    return jnp.concatenate([jnp.dot(block, mirror, preferred_element_type=f32) for block in blocks], axis=1)


def lanes_at(block, count):
    return pl.ds(pl.multiple_of(block * LANES, LANES), count * LANES)


def channel_columns(taps_ref, skip_ref):
    taps = taps_ref.shape[0]
    rows = [taps_ref[i] for i in range(taps)] + [skip_ref[...][None, :]]
    channels = skip_ref.shape[0]
    rows.append(jnp.zeros((LANES - 3 * taps - 1, channels), f32))
    return jnp.transpose(jnp.concatenate(rows, axis=0))


def place_slots(me, local_blocks, slots, store):
    for step, slot in enumerate(slots):
        store(lanes_at(jnp.bitwise_xor(me, step) * local_blocks, local_blocks), slot)


def start_rows(source_ref, start, held, arrived):
    copies = []
    chunk = held.shape[0] // arrived.shape[0]
    for index in range(arrived.shape[0]):
        rows = pl.ds(pl.multiple_of(start + index * chunk, chunk), chunk)
        copies.append(
            pltpu.make_async_copy(source_ref.at[rows], held.at[index * chunk : (index + 1) * chunk], arrived.at[index])
        )
        copies[-1].start()
    return copies


def split_blocks(total, chip, rows, send, kept, columns):
    for index in range(total.shape[0] // (2 * rows)):
        place = slice(index * rows, (index + 1) * rows)
        for target, bit in ((send, 1 - chip % 2), (kept, chip % 2)):
            source = pl.ds(pl.multiple_of((2 * index + bit) * rows, 8), rows)
            target[place, columns] = total[source].astype(target.dtype)


def write_out(pairs, columns, left, first):
    copies = []
    for index, (source, target) in enumerate(pairs):
        copies.append(pltpu.make_async_copy(source.at[:, columns], target.at[:, columns], left.at[first + index]))
        copies[-1].start()
    return copies


def project_kernel(
    chips, core_ref, chip_ref, hidden_ref, other_ref, weight_ref, other_weight_ref,
    send_ref, kept_ref, weight, arrived, other_weight, other_arrived, total, send, kept, left, hidden, other, came,
):
    operands = [
        pltpu.make_async_copy(hidden_ref, hidden, came.at[0]),
        pltpu.make_async_copy(other_ref, other, came.at[1]),
    ]
    for copy in operands:
        copy.start()
    half = weight.shape[0]
    start = core_ref[0] * half
    copies = start_rows(weight_ref, start, weight, arrived)
    other_copies = start_rows(other_weight_ref, start, other_weight, other_arrived)
    rows = total.shape[0] // chips
    chunk = half // len(copies)
    for copy in operands:
        copy.wait()
    leaving = []
    for index in range(len(copies)):
        columns = slice(index * chunk, (index + 1) * chunk)
        copies[index].wait()
        other_copies[index].wait()
        total[...] = lax.dot_general(
            hidden[...], weight[columns], CONTRACT_LAST, preferred_element_type=f32
        ) + lax.dot_general(other[...], other_weight[columns], CONTRACT_LAST, preferred_element_type=f32)
        split_blocks(total, chip_ref[0], rows, send, kept, columns)
        leaving += write_out(((send, send_ref), (kept, kept_ref)), columns, left, 2 * index)
    for copy in leaving:
        copy.wait()


def assemble_kernel(rows, steps, chip_ref, core_ref, *refs):
    out_ref = refs[-1]
    columns = refs[0].shape[1]
    for index, held in enumerate(steps + steps):
        side = core_ref[0] if index < len(steps) else 1 - core_ref[0]
        for slot, step in enumerate(held):
            place = pl.ds(pl.multiple_of(jnp.bitwise_xor(chip_ref[0], step) * rows, rows), rows)
            at = (place, pl.ds(pl.multiple_of(side * columns, columns), columns))
            out_ref[at] = refs[index][slot * rows : (slot + 1) * rows]


def forward_kernel(shards, me_ref, *refs):
    slots = refs[:shards]
    letters_ref, gain_ref, weight_ref, taps_ref, skip_ref = refs[shards : shards + 5]
    hidden_ref, mixed_ref, table_ref = refs[shards + 5 : shards + 8]
    normed, hot, filters, matrices, signal, exact, long_part, weight, arrived, table, left = refs[shards + 8 :]
    groups = filters.shape[0]
    local_rows = slots[0].shape[1]
    channels = table.shape[2]
    width = channels // groups
    local_blocks = local_rows // LANES
    blocks = shards * local_blocks
    length = blocks * LANES
    window = local_blocks + 1
    chunks = arrived.shape[0]
    chunk = weight.shape[1] // chunks
    taps = taps_ref.shape[0]
    me = me_ref[0]
    first = me * local_blocks

    copies = []
    for index in range(chunks):
        rows = slice(index * chunk, (index + 1) * chunk)
        copies.append(pltpu.make_async_copy(weight_ref.at[:, rows], weight.at[:, rows], arrived.at[index]))
        copies[-1].start()
    for index, slot in enumerate(slots):
        place = lanes_at(jnp.bitwise_xor(me, index) * local_blocks, local_blocks)
        filters[:, place] = slot[:groups]
        exact[0:1, place] = slot[groups : groups + 1]
    marks = one_hot(exact[0:1, :length].astype(jnp.int32), taps)
    hot[:, :length] = jnp.concatenate([marks, marks], axis=0).astype(bf16)
    hot[:, length:] = jnp.zeros((hot.shape[0], LANES), bf16)
    signal[:, :length] = jnp.zeros((channels, length), bf16)
    signal[:, 2 * length :] = jnp.zeros((channels, LANES), bf16)
    exact[:, length:] = jnp.zeros((channels, LANES), f32)
    values = letters_ref[...].astype(f32)
    inverse = lax.rsqrt(jnp.mean(values * values, axis=-1, keepdims=True) + 1e-06)
    normed[...] = (values * inverse * gain_ref[...][None, :]).astype(bf16)

    table[...] = jnp.zeros(table.shape, f32)
    share = groups // chunks

    def one_chunk(index, carry):
        rows = pl.ds(pl.multiple_of(index * chunk, chunk), chunk)
        pltpu.make_async_copy(weight_ref.at[:, rows], weight.at[:, rows], arrived.at[index]).wait()
        for offset in range(share):
            group = index * share + offset
            tiles = toeplitz_tiles(filters[pl.ds(group, 1), :], blocks, False)
            for q in range(blocks):
                matrices[group, (blocks - 1 - q) * LANES : (blocks - q) * LANES] = tiles[q]
        for part in range(3):
            table[part] += jnp.dot(normed[:, rows], weight[part, rows], preferred_element_type=f32)
        return carry

    lax.fori_loop(0, chunks, one_chunk, 0)
    table_copy = pltpu.make_async_copy(table, table_ref, left.at[0])
    table_copy.start()
    key_weights = tap_weights(taps_ref, table, 1)
    value_weights = tap_weights(taps_ref, table, 2)
    for start in range(0, channels, LANES):
        rows = slice(start, start + LANES)
        mixture = expand(key_weights[:, rows], hot[:, :length]) * expand(value_weights[:, rows], hot[:, :length])
        exact[rows, :length] = mixture
        signal[rows, length : 2 * length] = mixture.astype(bf16)

    def one_group(group, carry):
        rows = pl.ds(pl.multiple_of(group * width, width), width)
        left = jnp.concatenate([signal[rows, lanes_at(first + i + 1, blocks)] for i in range(window)], axis=0)
        result = jnp.dot(left, matrices[group], preferred_element_type=f32)
        for i in range(window):
            long_part[rows, i * LANES : (i + 1) * LANES] = result[i * width : (i + 1) * width]
        return carry

    lax.fori_loop(0, groups, one_group, 0, unroll=4)
    columns = channel_columns(taps_ref, skip_ref)
    mixed = columns[:, 3 * taps : 3 * taps + 1] * exact[:, lanes_at(first, window)] + long_part[...]
    long_part[...] = mixed
    mixed_copy = pltpu.make_async_copy(long_part, mixed_ref, left.at[1])
    mixed_copy.start()
    queries = expand(tap_weights(taps_ref, table, 0), hot[:, lanes_at(first, local_blocks)])
    hidden_ref[...] = jnp.transpose(queries * mixed[:, :local_rows]).astype(bf16)
    table_copy.wait()
    mixed_copy.wait()


def backward_kernel(shards, me_ref, core_ref, *refs):
    slots, grad_slots = refs[:shards], refs[shards : 2 * shards]
    table_ref, taps_ref, skip_ref, mixed_ref, output_grad_ref, hidden_ref, out_ref = refs[2 * shards : 2 * shards + 7]
    piece_refs = refs[2 * shards + 7 : 3 * shards + 6]
    hot, filters, grads, signal, exact, long_part, pieces, came, left = refs[3 * shards + 6 :]
    me = me_ref[0]
    share = output_grad_ref.shape[1] // shards
    part = share // 2
    incoming = []
    for step in range(1, shards):
        start = jnp.bitwise_xor(me, step) * share + core_ref[0] * part
        source = output_grad_ref.at[:, pl.ds(pl.multiple_of(start, part), part)]
        slot = pieces.at[step - 1]
        incoming.append(pltpu.make_async_copy(source, slot.at[:, :part], came.at[2 * step - 2]))
        incoming.append(pltpu.make_async_copy(hidden_ref, slot.at[:, part:], came.at[2 * step - 1]))
    for copy in incoming:
        copy.start()
    groups = filters.shape[0]
    local_rows = slots[0].shape[1]
    channels = table_ref.shape[2]
    width = channels // groups
    local_blocks = local_rows // LANES
    blocks = shards * local_blocks
    length = blocks * LANES
    window = local_blocks + 1
    taps = taps_ref.shape[0]

    for step in range(shards):
        place = lanes_at(jnp.bitwise_xor(me, step) * local_blocks, local_blocks)
        exact[0:1, place] = slots[step][groups : groups + 1]
        filters[:, place] = reverse_blocks(slots[step][:groups])
        grads[:, place] = grad_slots[step][...]
    grads[:, length:] = jnp.zeros((channels, LANES), bf16)
    marks = one_hot(exact[0:1, :length].astype(jnp.int32), taps)
    hot[:, :length] = jnp.concatenate([marks, marks], axis=0).astype(bf16)
    hot[:, length:] = jnp.zeros((hot.shape[0], LANES), bf16)

    signal[:, length:] = jnp.zeros((channels, length + LANES), bf16)
    exact[:, length:] = jnp.zeros((channels, LANES), f32)
    query_weights = tap_weights(taps_ref, table_ref, 0)
    for start in range(0, channels, LANES):
        rows = slice(start, start + LANES)
        mixed_grad = expand(query_weights[:, rows], hot[:, :length]) * grads[rows, :length].astype(f32)
        exact[rows, :length] = mixed_grad
        signal[rows, :length] = mixed_grad.astype(bf16)

    for copy in incoming:
        copy.wait()
    outgoing = []
    for step in range(1, shards):
        outgoing.append(pltpu.make_async_copy(pieces.at[step - 1], piece_refs[step - 1], left.at[step - 1]))
        outgoing[-1].start()
    first = me * local_blocks

    def one_group(group, carry):
        matrix = jnp.concatenate(toeplitz_tiles(filters[pl.ds(group, 1), :], blocks, True), axis=0)
        rows = pl.ds(pl.multiple_of(group * width, width), width)
        left = jnp.concatenate([signal[rows, lanes_at(first + i, blocks)] for i in range(window)], axis=0)
        result = jnp.dot(left, matrix, preferred_element_type=f32)
        for i in range(window):
            long_part[rows, i * LANES : (i + 1) * LANES] = result[i * width : (i + 1) * width]
        return carry

    lax.fori_loop(0, groups, one_group, 0, unroll=4)
    own = lanes_at(first, window)
    columns = channel_columns(taps_ref, skip_ref)
    mixture_grad = columns[:, 3 * taps : 3 * taps + 1] * exact[:, own] + long_part[...]
    span = window * LANES
    for part in range(3):
        if part == 0:
            feature_grad = grads[:, own].astype(f32) * mixed_ref[...]
        else:
            other = expand(tap_weights(taps_ref, table_ref, 3 - part), hot[:, own])
            feature_grad = mixture_grad * other
        total = columns[:, part : part + 1] * feature_grad
        for tap in range(1, taps):
            column = 3 * tap + part
            total = total + columns[:, column : column + 1] * pltpu.roll(feature_grad, span - tap, axis=1)
        out_ref[part] = jnp.transpose(total[:, :local_rows]).astype(bf16)
    for copy in outgoing:
        copy.wait()


def hidden_grad_kernel(grad_ref, weight_ref, out_ref, grad, weight, total, arrived):
    chunks = arrived.shape[0] // 2
    chunk = weight.shape[0] // chunks
    copies = []
    for index in range(chunks):
        part = slice(index * chunk, (index + 1) * chunk)
        copies.append(pltpu.make_async_copy(grad_ref.at[:, part], grad.at[:, part], arrived.at[2 * index]))
        copies.append(pltpu.make_async_copy(weight_ref.at[part], weight.at[part], arrived.at[2 * index + 1]))
    for copy in copies:
        copy.start()
    for index in range(chunks):
        part = slice(index * chunk, (index + 1) * chunk)
        copies[2 * index].wait()
        copies[2 * index + 1].wait()
        term = jnp.dot(grad[:, part], weight[part], preferred_element_type=f32)
        total[...] = term if index == 0 else total[...] + term
    out_ref[...] = jnp.transpose(total[...]).astype(bf16)


def input_grad_kernel(
    chips, core_ref, chip_ref, grad_ref, other_grad_ref, weight_ref, other_weight_ref,
    send_ref, kept_ref, weight, other_weight, arrived, total, send, kept, left,
):
    half = weight.shape[1]
    chunks = arrived.shape[0] // 2
    chunk = half // chunks
    copies = []
    for index in range(chunks):
        columns = slice(index * chunk, (index + 1) * chunk)
        source = pl.ds(pl.multiple_of(core_ref[0] * half + index * chunk, chunk), chunk)
        pair = (
            pltpu.make_async_copy(weight_ref.at[:, source], weight.at[:, columns], arrived.at[2 * index]),
            pltpu.make_async_copy(other_weight_ref.at[:, source], other_weight.at[:, columns], arrived.at[2 * index + 1]),
        )
        for copy in pair:
            copy.start()
        copies.append(pair)
    rows = total.shape[0] // chips
    leaving = []
    for index in range(chunks):
        columns = slice(index * chunk, (index + 1) * chunk)
        value = None
        for copy, grad, held in zip(copies[index], (grad_ref, other_grad_ref), (weight, other_weight)):
            copy.wait()
            for part in range(3):
                term = lax.dot_general(grad[part], held[part, columns], CONTRACT_LAST, preferred_element_type=f32)
                value = term if value is None else value + term
        total[...] = value
        split_blocks(total, chip_ref[0], rows, send, kept, columns)
        leaving += write_out(((send, send_ref), (kept, kept_ref)), columns, left, 2 * index)
    for copy in leaving:
        copy.wait()


def weight_grad_kernel(shards, me_ref, core_ref, grad_ref, hidden_ref, *refs):
    mine, theirs = refs[: shards - 1], refs[shards - 1 : 2 * shards - 2]
    out_ref, own, arrived = refs[2 * shards - 2 :]
    share = own.shape[1]
    part = share // 2
    source = grad_ref.at[:, pl.ds(pl.multiple_of(me_ref[0] * share, share), share)]
    copy = pltpu.make_async_copy(source, own, arrived)
    copy.start()
    for pieces, side in ((mine, core_ref[0]), (theirs, 1 - core_ref[0])):
        total = None
        for piece, with_hidden in zip(pieces, mine):
            term = expand(piece[:, :part], with_hidden[:, part:])
            total = term if total is None else total + term
        if pieces is mine:
            copy.wait()
        place = pl.ds(pl.multiple_of(side * part, part), part)
        out_ref[place, :] = total + expand(own[:, place], hidden_ref[...])


def pack_kernel(filters_ref, ids_ref, out_ref):
    groups = filters_ref.shape[0]
    out_ref[:groups] = filters_ref[...]
    out_ref[groups:] = jnp.broadcast_to(ids_ref[...].astype(f32)[None, :], (8, ids_ref.shape[0]))


def in_vmem(count):
    return [pl.BlockSpec(memory_space=pltpu.VMEM)] * count


SMEM_SPEC = pl.BlockSpec(memory_space=pltpu.SMEM)
ANY_SPEC = pl.BlockSpec(memory_space=pl.ANY)
VMEM_SPEC = pl.BlockSpec(memory_space=pltpu.VMEM)
CHUNKS = 8


def params():
    return pltpu.CompilerParams(vmem_limit_bytes=VMEM_BYTES)


LARGE_COST = pl.CostEstimate(flops=20_000_000_000, bytes_accessed=10_000_000, transcendentals=0)
SMALL_COST = pl.CostEstimate(flops=1000, bytes_accessed=1000, transcendentals=0)


def insert_kernel(rows, steps, chip_ref, core_ref, own_ref, theirs_ref, base_ref, out_ref, moved):
    columns = own_ref.shape[1]
    copies = []
    for index, step in enumerate(steps):
        place = pl.ds(pl.multiple_of(jnp.bitwise_xor(chip_ref[0], step) * rows, rows), rows)
        for which, source in enumerate((own_ref, theirs_ref)):
            side = core_ref[0] if which == 0 else 1 - core_ref[0]
            target = out_ref.at[place, pl.ds(pl.multiple_of(side * columns, columns), columns)]
            part = source.at[index * rows : (index + 1) * rows]
            copies.append(pltpu.make_async_copy(part, target, moved.at[2 * index + which]))
            copies[-1].start()
    for copy in copies:
        copy.wait()


def run_insert(steps, chip, core, own, theirs, base):
    return pl.pallas_call(
        functools.partial(insert_kernel, own.shape[0] // len(steps), steps),
        out_shape=jax.ShapeDtypeStruct(base.shape, base.dtype),
        in_specs=[SMEM_SPEC, SMEM_SPEC, VMEM_SPEC, VMEM_SPEC, ANY_SPEC],
        out_specs=ANY_SPEC,
        scratch_shapes=[pltpu.SemaphoreType.DMA((2 * len(steps),))],
        input_output_aliases={4: 0},
        compiler_params=params(),
        cost_estimate=SMALL_COST,
        name="insert",
    )(chip, core, own, theirs, base)


def run_assemble(chips, steps, chip, core, own, theirs):
    rows, columns = own[0].shape
    return pl.pallas_call(
        functools.partial(assemble_kernel, rows, steps),
        out_shape=jax.ShapeDtypeStruct((chips * rows, 2 * columns), bf16),
        in_specs=[SMEM_SPEC, SMEM_SPEC] + in_vmem(2 * len(own)),
        out_specs=VMEM_SPEC,
        compiler_params=params(),
        cost_estimate=SMALL_COST,
        name="assemble",
    )(chip, core, *own, *theirs)


def run_forward(me, slots, embed_table, norm_gain, weight, taps, skip_gain):
    shards = len(slots)
    local_rows = slots[0].shape[1]
    _, width, channels = weight.shape
    groups = slots[0].shape[0] - 8
    length = shards * local_rows
    span = local_rows + LANES
    return pl.pallas_call(
        functools.partial(forward_kernel, shards),
        grid=(1,),
        out_shape=(
            jax.ShapeDtypeStruct((local_rows, channels), bf16),
            jax.ShapeDtypeStruct((channels, span), f32),
            jax.ShapeDtypeStruct((3, IDS, channels), f32),
        ),
        in_specs=[SMEM_SPEC]
        + in_vmem(shards)
        + [pl.BlockSpec((IDS, width), lambda step: (FIRST_ID // IDS, 0)), VMEM_SPEC, ANY_SPEC, VMEM_SPEC, VMEM_SPEC],
        out_specs=(VMEM_SPEC, ANY_SPEC, ANY_SPEC),
        scratch_shapes=[
            pltpu.VMEM((IDS, width), bf16),
            pltpu.VMEM((2 * taps.shape[0] * IDS, length + LANES), bf16),
            pltpu.VMEM((groups, length), f32),
            pltpu.VMEM((groups, length, LANES), bf16),
            pltpu.VMEM((channels, 2 * length + LANES), bf16),
            pltpu.VMEM((channels, length + LANES), f32),
            pltpu.VMEM((channels, span), f32),
            pltpu.VMEM(weight.shape, bf16),
            pltpu.SemaphoreType.DMA((CHUNKS,)),
            pltpu.VMEM((3, IDS, channels), f32),
            pltpu.SemaphoreType.DMA((2,)),
        ],
        compiler_params=params(),
        cost_estimate=LARGE_COST,
        name="forward_conv",
    )(me, *slots, embed_table, norm_gain, weight, taps, skip_gain)


def run_project(core, chip, chips, hidden, other_hidden, weight, other_weight):
    rows, channels = hidden.shape
    half = weight.shape[0] // 2
    return pl.pallas_call(
        functools.partial(project_kernel, chips),
        out_shape=(jax.ShapeDtypeStruct((rows // 2, half), bf16), jax.ShapeDtypeStruct((rows // 2, half), f32)),
        in_specs=[SMEM_SPEC, SMEM_SPEC] + [ANY_SPEC] * 4,
        out_specs=(ANY_SPEC, ANY_SPEC),
        scratch_shapes=[
            pltpu.VMEM((half, channels), bf16),
            pltpu.SemaphoreType.DMA((4,)),
            pltpu.VMEM((half, channels), bf16),
            pltpu.SemaphoreType.DMA((4,)),
            pltpu.VMEM((rows, half // 4), f32),
            pltpu.VMEM((rows // 2, half), bf16),
            pltpu.VMEM((rows // 2, half), f32),
            pltpu.SemaphoreType.DMA((8,)),
            pltpu.VMEM((rows, channels), bf16),
            pltpu.VMEM((rows, channels), bf16),
            pltpu.SemaphoreType.DMA((2,)),
        ],
        compiler_params=params(),
        cost_estimate=SMALL_COST,
        name="project",
    )(core, chip, hidden, other_hidden, weight, other_weight)


def run_backward(me, core, slots, grads, table, taps, skip_gain, mixed, output_grad, hidden):
    shards = len(slots)
    local_rows = slots[0].shape[1]
    channels = table.shape[2]
    groups = slots[0].shape[0] - 8
    length = shards * local_rows
    span = local_rows + LANES
    part = output_grad.shape[1] // (2 * shards)
    return pl.pallas_call(
        functools.partial(backward_kernel, shards),
        out_shape=[jax.ShapeDtypeStruct((3, local_rows, channels), bf16)]
        + [jax.ShapeDtypeStruct((local_rows, part + channels), bf16)] * (shards - 1),
        in_specs=[SMEM_SPEC, SMEM_SPEC] + in_vmem(2 * shards + 4) + [ANY_SPEC, ANY_SPEC],
        out_specs=[VMEM_SPEC] + [ANY_SPEC] * (shards - 1),
        scratch_shapes=[
            pltpu.VMEM((2 * taps.shape[0] * IDS, length + LANES), bf16),
            pltpu.VMEM((groups, length), f32),
            pltpu.VMEM((channels, length + LANES), bf16),
            pltpu.VMEM((channels, 2 * length + LANES), bf16),
            pltpu.VMEM((channels, length + LANES), f32),
            pltpu.VMEM((channels, span), f32),
            pltpu.VMEM((shards - 1, local_rows, part + channels), bf16),
            pltpu.SemaphoreType.DMA((2 * shards - 2,)),
            pltpu.SemaphoreType.DMA((shards - 1,)),
        ],
        compiler_params=params(),
        cost_estimate=LARGE_COST,
        name="backward_conv",
    )(me, core, *slots, *grads, table, taps, skip_gain, mixed, output_grad, hidden)


def run_weight_grad(me, core, output_grad, hidden, mine, theirs):
    shards = len(mine) + 1
    rows, width = output_grad.shape
    share, channels = width // shards, hidden.shape[1]
    return pl.pallas_call(
        functools.partial(weight_grad_kernel, shards),
        out_shape=jax.ShapeDtypeStruct((share, channels), f32),
        in_specs=[SMEM_SPEC, SMEM_SPEC, ANY_SPEC] + in_vmem(2 * shards - 1),
        out_specs=VMEM_SPEC,
        scratch_shapes=[pltpu.VMEM((rows, share), bf16), pltpu.SemaphoreType.DMA],
        compiler_params=params(),
        cost_estimate=SMALL_COST,
        name="weight_grad",
    )(me, core, output_grad, hidden, *mine, *theirs)


def run_hidden_grad(output_grad, output_weight):
    rows, width = output_grad.shape
    channels = output_weight.shape[1]
    return pl.pallas_call(
        hidden_grad_kernel,
        out_shape=jax.ShapeDtypeStruct((channels, rows), bf16),
        in_specs=[ANY_SPEC, ANY_SPEC],
        out_specs=VMEM_SPEC,
        scratch_shapes=[
            pltpu.VMEM((rows, width), bf16),
            pltpu.VMEM((width, channels), bf16),
            pltpu.VMEM((rows, channels), f32),
            pltpu.SemaphoreType.DMA((2 * CHUNKS,)),
        ],
        compiler_params=params(),
        cost_estimate=SMALL_COST,
        name="hidden_grad",
    )(output_grad, output_weight)


def run_input_grad(core, chip, chips, grad, other_grad, weight, other_weight):
    _, rows, channels = grad.shape
    half = weight.shape[1] // 2
    return pl.pallas_call(
        functools.partial(input_grad_kernel, chips),
        out_shape=(jax.ShapeDtypeStruct((rows // 2, half), bf16), jax.ShapeDtypeStruct((rows // 2, half), f32)),
        in_specs=[SMEM_SPEC, SMEM_SPEC, VMEM_SPEC, VMEM_SPEC, ANY_SPEC, ANY_SPEC],
        out_specs=(ANY_SPEC, ANY_SPEC),
        scratch_shapes=[
            pltpu.VMEM((3, half, channels), bf16),
            pltpu.VMEM((3, half, channels), bf16),
            pltpu.SemaphoreType.DMA((8,)),
            pltpu.VMEM((rows, half // 4), f32),
            pltpu.VMEM((rows // 2, half), bf16),
            pltpu.VMEM((rows // 2, half), f32),
            pltpu.SemaphoreType.DMA((8,)),
        ],
        compiler_params=params(),
        cost_estimate=SMALL_COST,
        name="input_grad",
    )(core, chip, grad, other_grad, weight, other_weight)


def run_pack(filters, ids):
    return pl.pallas_call(
        pack_kernel,
        out_shape=jax.ShapeDtypeStruct((filters.shape[0] + 8, filters.shape[1]), f32),
        in_specs=[VMEM_SPEC, VMEM_SPEC],
        out_specs=VMEM_SPEC,
        compiler_params=params(),
        cost_estimate=SMALL_COST,
        name="pack",
    )(filters, ids)


def ctx_exchange(value, step):
    count = lax.axis_size("ctx")
    return lax.ppermute(value, "ctx", [(i, i ^ step) for i in range(count)])


def gather_ctx(value):
    return [value] + [ctx_exchange(value, step) for step in range(1, lax.axis_size("ctx"))]


def tp_exchange(value, mask):
    count = lax.axis_size("tp")
    return lax.ppermute(value, "tp", [(i, i ^ mask) for i in range(count)])


def together(*values):
    return lax.optimization_barrier(values)


def pick(value, index, axis=0):
    return lax.dynamic_index_in_dim(value, index, axis=axis, keepdims=False)


def scalar_array(value):
    return jnp.reshape(value, (1,)).astype(jnp.int32)


def body(
    token_ids,
    embed_table,
    norm_gain,
    input_weight,
    short_weight,
    filters,
    skip_gain,
    output_weight,
    output_grad,
):
    shards = lax.axis_size("ctx")
    chips = lax.axis_size("tp") // 2
    hops = chips - 1
    me = lax.axis_index("ctx")
    core = lax.axis_index("tp") % 2
    chip = lax.axis_index("tp") // 2
    local_rows = token_ids.shape[0]
    width, channels = output_weight.shape
    me_tie, core_tie, chip_tie = scalar_array(me), scalar_array(core), scalar_array(chip)
    weight = jnp.transpose(input_weight, (1, 0, 2))

    half = width // 2
    levels = chips.bit_length() - 1
    block_rows = local_rows // chips
    packed = run_pack(filters, token_ids)
    slots = gather_ctx(packed)
    other_weight, other_input = tp_exchange(output_weight, 1), tp_exchange(weight, 1)
    hidden_grad = run_hidden_grad(output_grad, output_weight)
    arrived, hidden_grad, me_tie = together(slots[1:], hidden_grad, me_tie)
    slots = [packed] + arrived
    grad_slots = gather_ctx(hidden_grad)

    hidden, mixed, table = run_forward(
        me_tie, slots, embed_table, norm_gain, weight, short_weight, skip_gain
    )
    hidden, grad_slots, other_weight = together(hidden, grad_slots, other_weight)
    send, kept = run_project(
        core_tie, chip_tie, chips, hidden, tp_exchange(hidden, 1), output_weight, other_weight
    )

    def pairs(value, which):
        return pick(value.reshape((value.shape[0] // 2, 2) + value.shape[1:]), which, 1)

    def leaving(terms, bit):
        which = 1 - (chip >> bit & 1)
        return sum(pairs(term, which).astype(f32) for term in terms).astype(bf16)

    def keep(terms, bit):
        which = chip >> bit & 1
        return [pairs(term, which) for term in terms]

    blocks = (chips // 2, block_rows, half)
    near, others = range(1, shards // 2 + 1), range(shards // 2 + 1, shards)
    send, kept, me_tie = together(send, kept, me_tie)
    out_arrived = tp_exchange(send, 2)
    projection_grad, *pieces = run_backward(
        me_tie, core_tie, slots, grad_slots, table, short_weight, skip_gain, mixed, output_grad, hidden
    )
    projection_grad, pieces = together(projection_grad, pieces)
    other_grad = tp_exchange(projection_grad, 1)
    near_pieces = [ctx_exchange(pieces[step - 1], step) for step in near]
    grad_send, grad_kept = run_input_grad(
        core_tie, chip_tie, chips, projection_grad, other_grad, weight, other_input
    )
    out_terms = [kept.reshape(blocks), out_arrived.reshape(blocks)]
    for bit in range(1, levels):
        out_terms = keep(out_terms, bit) + [tp_exchange(leaving(out_terms, bit), 2 << bit)]
    grad_send, grad_kept, pieces, near_pieces, late_ids = together(
        grad_send, grad_kept, pieces, near_pieces, token_ids
    )
    grad_arrived = tp_exchange(grad_send, 2)
    far_pieces = [ctx_exchange(pieces[step - 1], step) for step in others]

    own_ids = lax.dynamic_slice_in_dim(late_ids, chip * block_rows, block_rows, axis=0)
    own_hot = (own_ids[:, None] == jnp.arange(FIRST_ID, FIRST_ID + IDS)[None, :]).astype(bf16)
    own_letters = lax.dynamic_slice(embed_table, (FIRST_ID, core * half), (IDS, half))
    own_tokens = jnp.dot(own_hot, own_letters, preferred_element_type=f32)
    block = sum(term.astype(f32) for term in out_terms).reshape(block_rows, half)
    block = (own_tokens + block).astype(bf16)
    line, steps = [block], [[0]]
    for level in range(levels - 1):
        mask = chips >> level + 1
        held = line[0] if level == 0 else jnp.concatenate(line, axis=0)
        came = tp_exchange(held, 2 * mask)
        line.append(came)
        steps.append([step ^ mask for group in steps for step in group])
    grad_arrived, far_pieces = together(grad_arrived, far_pieces)
    grad_terms = [grad_kept.reshape(blocks), grad_arrived.reshape(blocks)]
    held = jnp.concatenate(line, axis=0)
    for bit in range(1, levels):
        grad_terms = keep(grad_terms, bit) + [tp_exchange(leaving(grad_terms, bit), 2 << bit)]
    came = tp_exchange(held, 2)
    came_steps = [step ^ 1 for group in steps for step in group]

    base = run_assemble(chips, steps, chip_tie, core_tie, line, [tp_exchange(value, 1) for value in line])
    mine = near_pieces + far_pieces
    output_weight_grad = run_weight_grad(
        me_tie, core_tie, output_grad, hidden, mine, [tp_exchange(value, 1) for value in mine]
    )
    kept_sum = sum(term.astype(f32) for term in grad_terms[:-1])
    base, output_weight_grad, came = together(base, output_weight_grad, came)
    output_weight_grad, kept_sum, last = together(output_weight_grad, kept_sum, grad_terms[-1])
    total = (kept_sum + last.astype(f32)).reshape(2, block_rows // 2, half)
    my_rows, their_rows = pick(total, core), pick(total, 1 - core)
    other_columns = tp_exchange(their_rows, 1)
    block_output = run_insert(came_steps, chip_tie, core_tie, came, tp_exchange(came, 1), base)
    normed_grad = jnp.where(
        core == 0,
        jnp.concatenate([my_rows, other_columns], axis=1),
        jnp.concatenate([other_columns, my_rows], axis=1),
    )
    return (block_output, output_weight_grad, jnp.transpose(projection_grad, (1, 0, 2)), normed_grad)


def solution(mesh):
    in_specs = (
        P("ctx"),
        P(),
        P(),
        P(None, None, "tp"),
        P(None, None, "tp"),
        P("tp", "ctx"),
        P("tp"),
        P(None, "tp"),
        P("ctx", None),
    )
    out_specs = (P("ctx", None), P("ctx", "tp"), P("ctx", None, "tp"), P(("ctx", "tp"), None))
    return jax.shard_map(body, mesh=mesh, in_specs=in_specs, out_specs=out_specs, check_vma=False)
```

```python
import functools

import jax
import jax.numpy as jnp
from jax import lax
from jax.experimental import pallas as pl
from jax.experimental.pallas import tpu as pltpu
from jax.sharding import PartitionSpec as P

LANES = 128
FIRST_ID = 64
IDS = 32
VMEM_BYTES = 56 * 1024 * 1024
f32 = jnp.float32
bf16 = jnp.bfloat16
CONTRACT_LAST = (((1,), (1,)), ((), ()))


def one_hot(ids, taps):
    length = ids.shape[1]
    lane = lax.broadcasted_iota(jnp.int32, (1, length), 1)
    code = lax.broadcasted_iota(jnp.int32, (IDS, length), 0) + FIRST_ID
    rows = []
    for tap in range(taps):
        moved = ids if tap == 0 else jnp.where(lane < tap, 0, pltpu.roll(ids, tap, axis=1))
        rows.append(jnp.where(code == moved, 1.0, 0.0))
    return jnp.concatenate(rows, axis=0)


def tap_weights(taps_ref, table_ref, part):
    table = table_ref[part]
    value = jnp.concatenate([taps_ref[i, part][None, :] * table for i in range(taps_ref.shape[0])], axis=0)
    high = value.astype(bf16).astype(f32)
    return jnp.concatenate([high, value - high], axis=0).astype(bf16)


def expand(weights, hot):
    return lax.dot_general(weights, hot, (((0,), (0,)), ((), ())), preferred_element_type=f32)


def toeplitz_tiles(row, blocks, mirrored):
    sub = lax.broadcasted_iota(jnp.int32, (LANES, LANES), 0)
    lane = lax.broadcasted_iota(jnp.int32, (LANES, LANES), 1)
    keep = lane <= sub if mirrored else lane >= sub
    before = jnp.zeros((LANES, LANES), f32)
    tiles = []
    for q in range(blocks):
        part = jnp.broadcast_to(row[:, LANES * q : LANES * (q + 1)], (LANES, LANES))
        turned = pltpu.roll(part, 1 if mirrored else 0, 1, stride=1, stride_axis=0)
        tiles.append(jnp.where(keep, turned, before).astype(bf16))
        before = turned
    return tiles


def reverse_blocks(value):
    sub = lax.broadcasted_iota(jnp.int32, (LANES, LANES), 0)
    lane = lax.broadcasted_iota(jnp.int32, (LANES, LANES), 1)
    mirror = jnp.where(sub + lane == LANES - 1, 1.0, 0.0).astype(bf16)
    blocks = [value[:, start : start + LANES].astype(bf16) for start in range(0, value.shape[1], LANES)]
    return jnp.concatenate([jnp.dot(block, mirror, preferred_element_type=f32) for block in blocks], axis=1)


def lanes_at(block, count):
    return pl.ds(pl.multiple_of(block * LANES, LANES), count * LANES)


def channel_columns(taps_ref, skip_ref):
    taps = taps_ref.shape[0]
    rows = [taps_ref[i] for i in range(taps)] + [skip_ref[...][None, :]]
    channels = skip_ref.shape[0]
    rows.append(jnp.zeros((LANES - 3 * taps - 1, channels), f32))
    return jnp.transpose(jnp.concatenate(rows, axis=0))


def place_slots(me, local_blocks, slots, store):
    for step, slot in enumerate(slots):
        store(lanes_at(jnp.bitwise_xor(me, step) * local_blocks, local_blocks), slot)


def start_rows(source_ref, start, held, arrived):
    copies = []
    chunk = held.shape[0] // arrived.shape[0]
    for index in range(arrived.shape[0]):
        rows = pl.ds(pl.multiple_of(start + index * chunk, chunk), chunk)
        copies.append(
            pltpu.make_async_copy(source_ref.at[rows], held.at[index * chunk : (index + 1) * chunk], arrived.at[index])
        )
        copies[-1].start()
    return copies


def split_blocks(total, chip, rows, parts, columns):
    low, high = chip % 2, chip // 2 % 2
    for index in range(total.shape[0] // (4 * rows)):
        place = slice(index * rows, (index + 1) * rows)
        for target, first, second in zip(parts, (1 - low, 1 - low, low, low), (1 - high, high, 1 - high, high)):
            source = pl.ds(pl.multiple_of((4 * index + 2 * second + first) * rows, 8), rows)
            target[place, columns] = total[source].astype(target.dtype)


def write_out(sources, targets, columns, left, first):
    copies = []
    for index, (source, target) in enumerate(zip(sources, targets)):
        copies.append(pltpu.make_async_copy(source.at[:, columns], target.at[:, columns], left.at[first + index]))
        copies[-1].start()
    return copies


PARTS = 4


def part_shapes(rows, half):
    return [jax.ShapeDtypeStruct((rows // PARTS, half), kind) for kind in (bf16, bf16, f32, f32)]


def part_buffers(rows, half):
    return [pltpu.VMEM((rows // PARTS, half), kind) for kind in (bf16, bf16, f32, f32)]


def project_kernel(
    chips, core_ref, chip_ref, hidden_ref, other_ref, weight_ref, other_weight_ref, *refs
):
    out_refs, parts = refs[:PARTS], refs[PARTS : 2 * PARTS]
    weight, arrived, other_weight, other_arrived, total, left, hidden, other, came = refs[2 * PARTS :]
    operands = [
        pltpu.make_async_copy(hidden_ref, hidden, came.at[0]),
        pltpu.make_async_copy(other_ref, other, came.at[1]),
    ]
    for copy in operands:
        copy.start()
    half = weight.shape[0]
    start = core_ref[0] * half
    copies = start_rows(weight_ref, start, weight, arrived)
    other_copies = start_rows(other_weight_ref, start, other_weight, other_arrived)
    rows = total.shape[0] // chips
    chunk = half // len(copies)
    for copy in operands:
        copy.wait()
    leaving = []
    for index in range(len(copies)):
        columns = slice(index * chunk, (index + 1) * chunk)
        copies[index].wait()
        other_copies[index].wait()
        total[...] = lax.dot_general(
            hidden[...], weight[columns], CONTRACT_LAST, preferred_element_type=f32
        ) + lax.dot_general(other[...], other_weight[columns], CONTRACT_LAST, preferred_element_type=f32)
        split_blocks(total, chip_ref[0], rows, parts, columns)
        leaving += write_out(parts, out_refs, columns, left, PARTS * index)
    for copy in leaving:
        copy.wait()


def assemble_kernel(rows, steps, chip_ref, core_ref, *refs):
    out_ref = refs[-1]
    columns = refs[0].shape[1]
    for index, held in enumerate(steps + steps):
        side = core_ref[0] if index < len(steps) else 1 - core_ref[0]
        for slot, step in enumerate(held):
            place = pl.ds(pl.multiple_of(jnp.bitwise_xor(chip_ref[0], step) * rows, rows), rows)
            at = (place, pl.ds(pl.multiple_of(side * columns, columns), columns))
            out_ref[at] = refs[index][slot * rows : (slot + 1) * rows]


def forward_kernel(shards, me_ref, core_ref, *refs):
    slots = refs[:shards]
    letters_ref, gain_ref, weight_ref, taps_ref, skip_ref, output_grad_ref = refs[shards : shards + 6]
    hidden_ref, mixed_ref, table_ref = refs[shards + 6 : shards + 9]
    piece_refs = refs[shards + 9 : 2 * shards + 8]
    normed, hot, filters, matrices, signal, exact, long_part, weight, arrived, table, left, pieces, came, pieces_left = refs[
        2 * shards + 8 :
    ]
    groups = filters.shape[0]
    local_rows = slots[0].shape[1]
    channels = table.shape[2]
    width = channels // groups
    local_blocks = local_rows // LANES
    blocks = shards * local_blocks
    length = blocks * LANES
    window = local_blocks + 1
    chunks = arrived.shape[0]
    chunk = weight.shape[1] // chunks
    taps = taps_ref.shape[0]
    me = me_ref[0]
    first = me * local_blocks

    copies = []
    for index in range(chunks):
        rows = slice(index * chunk, (index + 1) * chunk)
        copies.append(pltpu.make_async_copy(weight_ref.at[:, rows], weight.at[:, rows], arrived.at[index]))
        copies[-1].start()
    share = output_grad_ref.shape[1] // shards
    part = share // 2
    incoming = []
    for step in range(1, shards):
        start = jnp.bitwise_xor(me, step) * share + core_ref[0] * part
        source = output_grad_ref.at[:, pl.ds(pl.multiple_of(start, part), part)]
        incoming.append(pltpu.make_async_copy(source, pieces.at[step - 1, :, :part], came.at[step - 1]))
        incoming[-1].start()
    for index, slot in enumerate(slots):
        place = lanes_at(jnp.bitwise_xor(me, index) * local_blocks, local_blocks)
        filters[:, place] = slot[:groups]
        exact[0:1, place] = slot[groups : groups + 1]
    marks = one_hot(exact[0:1, :length].astype(jnp.int32), taps)
    hot[:, :length] = jnp.concatenate([marks, marks], axis=0).astype(bf16)
    hot[:, length:] = jnp.zeros((hot.shape[0], LANES), bf16)
    signal[:, :length] = jnp.zeros((channels, length), bf16)
    signal[:, 2 * length :] = jnp.zeros((channels, LANES), bf16)
    exact[:, length:] = jnp.zeros((channels, LANES), f32)
    values = letters_ref[...].astype(f32)
    inverse = lax.rsqrt(jnp.mean(values * values, axis=-1, keepdims=True) + 1e-06)
    normed[...] = (values * inverse * gain_ref[...][None, :]).astype(bf16)

    table[...] = jnp.zeros(table.shape, f32)
    per_chunk = groups // chunks

    def one_chunk(index, carry):
        rows = pl.ds(pl.multiple_of(index * chunk, chunk), chunk)
        pltpu.make_async_copy(weight_ref.at[:, rows], weight.at[:, rows], arrived.at[index]).wait()
        for offset in range(per_chunk):
            group = index * per_chunk + offset
            tiles = toeplitz_tiles(filters[pl.ds(group, 1), :], blocks, False)
            for q in range(blocks):
                matrices[group, (blocks - 1 - q) * LANES : (blocks - q) * LANES] = tiles[q]
        for part in range(3):
            table[part] += jnp.dot(normed[:, rows], weight[part, rows], preferred_element_type=f32)
        return carry

    lax.fori_loop(0, chunks, one_chunk, 0)
    table_copy = pltpu.make_async_copy(table, table_ref, left.at[0])
    table_copy.start()
    key_weights = tap_weights(taps_ref, table, 1)
    value_weights = tap_weights(taps_ref, table, 2)
    for start in range(0, channels, LANES):
        rows = slice(start, start + LANES)
        mixture = expand(key_weights[:, rows], hot[:, :length]) * expand(value_weights[:, rows], hot[:, :length])
        exact[rows, :length] = mixture
        signal[rows, length : 2 * length] = mixture.astype(bf16)

    def one_group(group, carry):
        rows = pl.ds(pl.multiple_of(group * width, width), width)
        left = jnp.concatenate([signal[rows, lanes_at(first + i + 1, blocks)] for i in range(window)], axis=0)
        result = jnp.dot(left, matrices[group], preferred_element_type=f32)
        for i in range(window):
            long_part[rows, i * LANES : (i + 1) * LANES] = result[i * width : (i + 1) * width]
        return carry

    lax.fori_loop(0, groups, one_group, 0, unroll=8)
    columns = channel_columns(taps_ref, skip_ref)
    mixed = columns[:, 3 * taps : 3 * taps + 1] * exact[:, lanes_at(first, window)] + long_part[...]
    long_part[...] = mixed
    mixed_copy = pltpu.make_async_copy(long_part, mixed_ref, left.at[1])
    mixed_copy.start()
    queries = expand(tap_weights(taps_ref, table, 0), hot[:, lanes_at(first, local_blocks)])
    hidden = jnp.transpose(queries * mixed[:, :local_rows]).astype(bf16)
    hidden_ref[...] = hidden
    outgoing = []
    for step in range(1, shards):
        incoming[step - 1].wait()
        pieces[step - 1, :, part:] = hidden
        outgoing.append(pltpu.make_async_copy(pieces.at[step - 1], piece_refs[step - 1], pieces_left.at[step - 1]))
        outgoing[-1].start()
    for copy in outgoing:
        copy.wait()
    table_copy.wait()
    mixed_copy.wait()


def backward_kernel(shards, me_ref, *refs):
    slots, grad_slots = refs[:shards], refs[shards : 2 * shards]
    table_ref, taps_ref, skip_ref, mixed_ref, out_ref = refs[2 * shards : 2 * shards + 5]
    hot, filters, grads, signal, exact, long_part = refs[2 * shards + 5 :]
    me = me_ref[0]
    groups = filters.shape[0]
    local_rows = slots[0].shape[1]
    channels = table_ref.shape[2]
    width = channels // groups
    local_blocks = local_rows // LANES
    blocks = shards * local_blocks
    length = blocks * LANES
    window = local_blocks + 1
    taps = taps_ref.shape[0]

    for step in range(shards):
        place = lanes_at(jnp.bitwise_xor(me, step) * local_blocks, local_blocks)
        exact[0:1, place] = slots[step][groups : groups + 1]
        filters[:, place] = reverse_blocks(slots[step][:groups])
        grads[:, place] = grad_slots[step][...]
    grads[:, length:] = jnp.zeros((channels, LANES), bf16)
    marks = one_hot(exact[0:1, :length].astype(jnp.int32), taps)
    hot[:, :length] = jnp.concatenate([marks, marks], axis=0).astype(bf16)
    hot[:, length:] = jnp.zeros((hot.shape[0], LANES), bf16)

    signal[:, length:] = jnp.zeros((channels, length + LANES), bf16)
    exact[:, length:] = jnp.zeros((channels, LANES), f32)
    query_weights = tap_weights(taps_ref, table_ref, 0)
    for start in range(0, channels, LANES):
        rows = slice(start, start + LANES)
        mixed_grad = expand(query_weights[:, rows], hot[:, :length]) * grads[rows, :length].astype(f32)
        exact[rows, :length] = mixed_grad
        signal[rows, :length] = mixed_grad.astype(bf16)

    first = me * local_blocks

    def one_group(group, carry):
        matrix = jnp.concatenate(toeplitz_tiles(filters[pl.ds(group, 1), :], blocks, True), axis=0)
        rows = pl.ds(pl.multiple_of(group * width, width), width)
        left = jnp.concatenate([signal[rows, lanes_at(first + i, blocks)] for i in range(window)], axis=0)
        result = jnp.dot(left, matrix, preferred_element_type=f32)
        for i in range(window):
            long_part[rows, i * LANES : (i + 1) * LANES] = result[i * width : (i + 1) * width]
        return carry

    lax.fori_loop(0, groups, one_group, 0, unroll=8)
    own = lanes_at(first, window)
    columns = channel_columns(taps_ref, skip_ref)
    mixture_grad = columns[:, 3 * taps : 3 * taps + 1] * exact[:, own] + long_part[...]
    span = window * LANES
    for part in range(3):
        if part == 0:
            feature_grad = grads[:, own].astype(f32) * mixed_ref[...]
        else:
            other = expand(tap_weights(taps_ref, table_ref, 3 - part), hot[:, own])
            feature_grad = mixture_grad * other
        total = columns[:, part : part + 1] * feature_grad
        for tap in range(1, taps):
            column = 3 * tap + part
            total = total + columns[:, column : column + 1] * pltpu.roll(feature_grad, span - tap, axis=1)
        out_ref[part] = jnp.transpose(total[:, :local_rows]).astype(bf16)


def hidden_grad_kernel(grad_ref, weight_ref, out_ref, grad, weight, total, arrived):
    chunks = arrived.shape[0] // 2
    chunk = weight.shape[0] // chunks
    copies = []
    for index in range(chunks):
        part = slice(index * chunk, (index + 1) * chunk)
        copies.append(pltpu.make_async_copy(grad_ref.at[:, part], grad.at[:, part], arrived.at[2 * index]))
        copies.append(pltpu.make_async_copy(weight_ref.at[part], weight.at[part], arrived.at[2 * index + 1]))
    for copy in copies:
        copy.start()
    for index in range(chunks):
        part = slice(index * chunk, (index + 1) * chunk)
        copies[2 * index].wait()
        copies[2 * index + 1].wait()
        term = jnp.dot(grad[:, part], weight[part], preferred_element_type=f32)
        total[...] = term if index == 0 else total[...] + term
    out_ref[...] = jnp.transpose(total[...]).astype(bf16)


def input_grad_kernel(
    chips, core_ref, chip_ref, grad_ref, other_grad_ref, weight_ref, other_weight_ref, *refs
):
    out_refs, parts = refs[:PARTS], refs[PARTS : 2 * PARTS]
    weight, other_weight, arrived, total, left = refs[2 * PARTS :]
    half = weight.shape[1]
    chunks = arrived.shape[0] // 2
    chunk = half // chunks
    copies = []
    for index in range(chunks):
        columns = slice(index * chunk, (index + 1) * chunk)
        source = pl.ds(pl.multiple_of(core_ref[0] * half + index * chunk, chunk), chunk)
        pair = (
            pltpu.make_async_copy(weight_ref.at[:, source], weight.at[:, columns], arrived.at[2 * index]),
            pltpu.make_async_copy(other_weight_ref.at[:, source], other_weight.at[:, columns], arrived.at[2 * index + 1]),
        )
        for copy in pair:
            copy.start()
        copies.append(pair)
    rows = total.shape[0] // chips
    leaving = []
    for index in range(chunks):
        columns = slice(index * chunk, (index + 1) * chunk)
        value = None
        for copy, grad, held in zip(copies[index], (grad_ref, other_grad_ref), (weight, other_weight)):
            copy.wait()
            for part in range(3):
                term = lax.dot_general(grad[part], held[part, columns], CONTRACT_LAST, preferred_element_type=f32)
                value = term if value is None else value + term
        total[...] = value
        split_blocks(total, chip_ref[0], rows, parts, columns)
        leaving += write_out(parts, out_refs, columns, left, PARTS * index)
    for copy in leaving:
        copy.wait()


def weight_grad_kernel(shards, me_ref, core_ref, grad_ref, hidden_ref, *refs):
    mine, theirs = refs[: shards - 1], refs[shards - 1 : 2 * shards - 2]
    out_ref, own, arrived = refs[2 * shards - 2 :]
    share = own.shape[1]
    part = share // 2
    source = grad_ref.at[:, pl.ds(pl.multiple_of(me_ref[0] * share, share), share)]
    copy = pltpu.make_async_copy(source, own, arrived)
    copy.start()
    for pieces, side in ((mine, core_ref[0]), (theirs, 1 - core_ref[0])):
        total = None
        for piece, with_hidden in zip(pieces, mine):
            term = expand(piece[:, :part], with_hidden[:, part:])
            total = term if total is None else total + term
        if pieces is mine:
            copy.wait()
        place = pl.ds(pl.multiple_of(side * part, part), part)
        out_ref[place, :] = total + expand(own[:, place], hidden_ref[...])


def pack_kernel(filters_ref, ids_ref, out_ref):
    groups = filters_ref.shape[0]
    out_ref[:groups] = filters_ref[...]
    out_ref[groups:] = jnp.broadcast_to(ids_ref[...].astype(f32)[None, :], (8, ids_ref.shape[0]))


def in_vmem(count):
    return [pl.BlockSpec(memory_space=pltpu.VMEM)] * count


SMEM_SPEC = pl.BlockSpec(memory_space=pltpu.SMEM)
ANY_SPEC = pl.BlockSpec(memory_space=pl.ANY)
VMEM_SPEC = pl.BlockSpec(memory_space=pltpu.VMEM)
CHUNKS = 8


def params():
    return pltpu.CompilerParams(vmem_limit_bytes=VMEM_BYTES)


LARGE_COST = pl.CostEstimate(flops=20_000_000_000, bytes_accessed=10_000_000, transcendentals=0)
SMALL_COST = pl.CostEstimate(flops=1000, bytes_accessed=1000, transcendentals=0)


def insert_kernel(rows, steps, chip_ref, core_ref, own_ref, theirs_ref, base_ref, out_ref, moved):
    columns = own_ref.shape[1]
    copies = []
    for index, step in enumerate(steps):
        place = pl.ds(pl.multiple_of(jnp.bitwise_xor(chip_ref[0], step) * rows, rows), rows)
        for which, source in enumerate((own_ref, theirs_ref)):
            side = core_ref[0] if which == 0 else 1 - core_ref[0]
            target = out_ref.at[place, pl.ds(pl.multiple_of(side * columns, columns), columns)]
            part = source.at[index * rows : (index + 1) * rows]
            copies.append(pltpu.make_async_copy(part, target, moved.at[2 * index + which]))
            copies[-1].start()
    for copy in copies:
        copy.wait()


def run_insert(steps, chip, core, own, theirs, base):
    return pl.pallas_call(
        functools.partial(insert_kernel, own.shape[0] // len(steps), steps),
        out_shape=jax.ShapeDtypeStruct(base.shape, base.dtype),
        in_specs=[SMEM_SPEC, SMEM_SPEC, VMEM_SPEC, VMEM_SPEC, ANY_SPEC],
        out_specs=ANY_SPEC,
        scratch_shapes=[pltpu.SemaphoreType.DMA((2 * len(steps),))],
        input_output_aliases={4: 0},
        compiler_params=params(),
        cost_estimate=SMALL_COST,
        name="insert",
    )(chip, core, own, theirs, base)


def run_assemble(chips, steps, chip, core, own, theirs):
    rows, columns = own[0].shape
    return pl.pallas_call(
        functools.partial(assemble_kernel, rows, steps),
        out_shape=jax.ShapeDtypeStruct((chips * rows, 2 * columns), bf16),
        in_specs=[SMEM_SPEC, SMEM_SPEC] + in_vmem(2 * len(own)),
        out_specs=VMEM_SPEC,
        compiler_params=params(),
        cost_estimate=SMALL_COST,
        name="assemble",
    )(chip, core, *own, *theirs)


def run_forward(me, core, slots, embed_table, norm_gain, weight, taps, skip_gain, output_grad):
    shards = len(slots)
    local_rows = slots[0].shape[1]
    _, width, channels = weight.shape
    groups = slots[0].shape[0] - 8
    length = shards * local_rows
    span = local_rows + LANES
    part = width // (2 * shards)
    return pl.pallas_call(
        functools.partial(forward_kernel, shards),
        grid=(1,),
        out_shape=(
            jax.ShapeDtypeStruct((local_rows, channels), bf16),
            jax.ShapeDtypeStruct((channels, span), f32),
            jax.ShapeDtypeStruct((3, IDS, channels), f32),
        )
        + (jax.ShapeDtypeStruct((local_rows, part + channels), bf16),) * (shards - 1),
        in_specs=[SMEM_SPEC, SMEM_SPEC]
        + in_vmem(shards)
        + [pl.BlockSpec((IDS, width), lambda step: (FIRST_ID // IDS, 0)), VMEM_SPEC, ANY_SPEC, VMEM_SPEC, VMEM_SPEC]
        + [ANY_SPEC],
        out_specs=(VMEM_SPEC,) + (ANY_SPEC,) * (shards + 1),
        scratch_shapes=[
            pltpu.VMEM((IDS, width), bf16),
            pltpu.VMEM((2 * taps.shape[0] * IDS, length + LANES), bf16),
            pltpu.VMEM((groups, length), f32),
            pltpu.VMEM((groups, length, LANES), bf16),
            pltpu.VMEM((channels, 2 * length + LANES), bf16),
            pltpu.VMEM((channels, length + LANES), f32),
            pltpu.VMEM((channels, span), f32),
            pltpu.VMEM(weight.shape, bf16),
            pltpu.SemaphoreType.DMA((CHUNKS,)),
            pltpu.VMEM((3, IDS, channels), f32),
            pltpu.SemaphoreType.DMA((2,)),
            pltpu.VMEM((shards - 1, local_rows, part + channels), bf16),
            pltpu.SemaphoreType.DMA((shards - 1,)),
            pltpu.SemaphoreType.DMA((shards - 1,)),
        ],
        compiler_params=params(),
        cost_estimate=LARGE_COST,
        name="forward_conv",
    )(me, core, *slots, embed_table, norm_gain, weight, taps, skip_gain, output_grad)


def run_project(core, chip, chips, hidden, other_hidden, weight, other_weight):
    rows, channels = hidden.shape
    half = weight.shape[0] // 2
    return pl.pallas_call(
        functools.partial(project_kernel, chips),
        out_shape=part_shapes(rows, half),
        in_specs=[SMEM_SPEC, SMEM_SPEC] + [ANY_SPEC] * 4,
        out_specs=[ANY_SPEC] * PARTS,
        scratch_shapes=part_buffers(rows, half)
        + [
            pltpu.VMEM((half, channels), bf16),
            pltpu.SemaphoreType.DMA((4,)),
            pltpu.VMEM((half, channels), bf16),
            pltpu.SemaphoreType.DMA((4,)),
            pltpu.VMEM((rows, half // 4), f32),
            pltpu.SemaphoreType.DMA((4 * PARTS,)),
            pltpu.VMEM((rows, channels), bf16),
            pltpu.VMEM((rows, channels), bf16),
            pltpu.SemaphoreType.DMA((2,)),
        ],
        compiler_params=params(),
        cost_estimate=SMALL_COST,
        name="project",
    )(core, chip, hidden, other_hidden, weight, other_weight)


def run_backward(me, slots, grads, table, taps, skip_gain, mixed):
    shards = len(slots)
    local_rows = slots[0].shape[1]
    channels = table.shape[2]
    groups = slots[0].shape[0] - 8
    length = shards * local_rows
    span = local_rows + LANES
    return pl.pallas_call(
        functools.partial(backward_kernel, shards),
        out_shape=jax.ShapeDtypeStruct((3, local_rows, channels), bf16),
        in_specs=[SMEM_SPEC] + in_vmem(2 * shards + 4),
        out_specs=VMEM_SPEC,
        scratch_shapes=[
            pltpu.VMEM((2 * taps.shape[0] * IDS, length + LANES), bf16),
            pltpu.VMEM((groups, length), f32),
            pltpu.VMEM((channels, length + LANES), bf16),
            pltpu.VMEM((channels, 2 * length + LANES), bf16),
            pltpu.VMEM((channels, length + LANES), f32),
            pltpu.VMEM((channels, span), f32),
        ],
        compiler_params=params(),
        cost_estimate=LARGE_COST,
        name="backward_conv",
    )(me, *slots, *grads, table, taps, skip_gain, mixed)


def run_weight_grad(me, core, output_grad, hidden, mine, theirs):
    shards = len(mine) + 1
    rows, width = output_grad.shape
    share, channels = width // shards, hidden.shape[1]
    return pl.pallas_call(
        functools.partial(weight_grad_kernel, shards),
        out_shape=jax.ShapeDtypeStruct((share, channels), f32),
        in_specs=[SMEM_SPEC, SMEM_SPEC, ANY_SPEC] + in_vmem(2 * shards - 1),
        out_specs=VMEM_SPEC,
        scratch_shapes=[pltpu.VMEM((rows, share), bf16), pltpu.SemaphoreType.DMA],
        compiler_params=params(),
        cost_estimate=SMALL_COST,
        name="weight_grad",
    )(me, core, output_grad, hidden, *mine, *theirs)


def run_hidden_grad(output_grad, output_weight):
    rows, width = output_grad.shape
    channels = output_weight.shape[1]
    return pl.pallas_call(
        hidden_grad_kernel,
        out_shape=jax.ShapeDtypeStruct((channels, rows), bf16),
        in_specs=[ANY_SPEC, ANY_SPEC],
        out_specs=VMEM_SPEC,
        scratch_shapes=[
            pltpu.VMEM((rows, width), bf16),
            pltpu.VMEM((width, channels), bf16),
            pltpu.VMEM((rows, channels), f32),
            pltpu.SemaphoreType.DMA((2 * CHUNKS,)),
        ],
        compiler_params=params(),
        cost_estimate=SMALL_COST,
        name="hidden_grad",
    )(output_grad, output_weight)


def run_input_grad(core, chip, chips, grad, other_grad, weight, other_weight):
    _, rows, channels = grad.shape
    half = weight.shape[1] // 2
    return pl.pallas_call(
        functools.partial(input_grad_kernel, chips),
        out_shape=part_shapes(rows, half),
        in_specs=[SMEM_SPEC, SMEM_SPEC, VMEM_SPEC, VMEM_SPEC, ANY_SPEC, ANY_SPEC],
        out_specs=[ANY_SPEC] * PARTS,
        scratch_shapes=part_buffers(rows, half)
        + [
            pltpu.VMEM((3, half, channels), bf16),
            pltpu.VMEM((3, half, channels), bf16),
            pltpu.SemaphoreType.DMA((8,)),
            pltpu.VMEM((rows, half // 4), f32),
            pltpu.SemaphoreType.DMA((4 * PARTS,)),
        ],
        compiler_params=params(),
        cost_estimate=SMALL_COST,
        name="input_grad",
    )(core, chip, grad, other_grad, weight, other_weight)


def run_pack(filters, ids):
    return pl.pallas_call(
        pack_kernel,
        out_shape=jax.ShapeDtypeStruct((filters.shape[0] + 8, filters.shape[1]), f32),
        in_specs=[VMEM_SPEC, VMEM_SPEC],
        out_specs=VMEM_SPEC,
        compiler_params=params(),
        cost_estimate=SMALL_COST,
        name="pack",
    )(filters, ids)


def ctx_exchange(value, step):
    count = lax.axis_size("ctx")
    return lax.ppermute(value, "ctx", [(i, i ^ step) for i in range(count)])


def gather_ctx(value):
    return [value] + [ctx_exchange(value, step) for step in range(1, lax.axis_size("ctx"))]


def tp_exchange(value, mask):
    count = lax.axis_size("tp")
    return lax.ppermute(value, "tp", [(i, i ^ mask) for i in range(count)])


def together(*values):
    return lax.optimization_barrier(values)


def pick(value, index, axis=0):
    return lax.dynamic_index_in_dim(value, index, axis=axis, keepdims=False)


def scalar_array(value):
    return jnp.reshape(value, (1,)).astype(jnp.int32)


def body(
    token_ids,
    embed_table,
    norm_gain,
    input_weight,
    short_weight,
    filters,
    skip_gain,
    output_weight,
    output_grad,
):
    shards = lax.axis_size("ctx")
    chips = lax.axis_size("tp") // 2
    hops = chips - 1
    me = lax.axis_index("ctx")
    core = lax.axis_index("tp") % 2
    chip = lax.axis_index("tp") // 2
    local_rows = token_ids.shape[0]
    width, channels = output_weight.shape
    me_tie, core_tie, chip_tie = scalar_array(me), scalar_array(core), scalar_array(chip)
    weight = jnp.transpose(input_weight, (1, 0, 2))

    half = width // 2
    levels = chips.bit_length() - 1
    block_rows = local_rows // chips
    packed = run_pack(filters, token_ids)
    slots = gather_ctx(packed)
    other_weight, other_input = tp_exchange(output_weight, 1), tp_exchange(weight, 1)
    hidden_grad = run_hidden_grad(output_grad, output_weight)
    arrived, hidden_grad, me_tie = together(slots[1:], hidden_grad, me_tie)
    slots = [packed] + arrived
    grad_slots = gather_ctx(hidden_grad)

    hidden, mixed, table, *pieces = run_forward(
        me_tie, core_tie, slots, embed_table, norm_gain, weight, short_weight, skip_gain, output_grad
    )
    hidden, grad_slots, other_weight = together(hidden, grad_slots, other_weight)
    project_parts = run_project(
        core_tie, chip_tie, chips, hidden, tp_exchange(hidden, 1), output_weight, other_weight
    )

    def pairs(value, which):
        return pick(value.reshape((value.shape[0] // 2, 2) + value.shape[1:]), which, 1)

    def leaving(terms, bit):
        which = 1 - (chip >> bit & 1)
        return sum(pairs(term, which).astype(f32) for term in terms).astype(bf16)

    def keep(terms, bit):
        which = chip >> bit & 1
        return [pairs(term, which) for term in terms]

    def halving(parts):
        leave, stay, kept_leave, kept_stay = parts
        arrived_leave = tp_exchange(leave, 2)
        arrived_stay = tp_exchange(stay, 2)
        return arrived_leave, arrived_stay, kept_leave, kept_stay

    def second_exchange(arrived_leave, kept_leave):
        return tp_exchange((kept_leave + arrived_leave.astype(f32)).astype(bf16), 4)

    def remaining(terms):
        terms = [term.reshape(chips // PARTS, block_rows, half) for term in terms]
        for bit in range(2, levels):
            terms = keep(terms, bit) + [tp_exchange(leaving(terms, bit), 2 << bit)]
        return terms

    near, others = range(1, shards // 2 + 1), range(shards // 2 + 1, shards)
    project_parts, me_tie, other_input = together(project_parts, me_tie, other_input)
    out_leave, out_stay, out_kept_leave, out_kept_stay = halving(project_parts)
    projection_grad = run_backward(me_tie, slots, grad_slots, table, short_weight, skip_gain, mixed)
    projection_grad, pieces = together(projection_grad, pieces)
    other_grad = tp_exchange(projection_grad, 1)
    near_pieces = [ctx_exchange(pieces[step - 1], step) for step in near]
    grad_parts = run_input_grad(
        core_tie, chip_tie, chips, projection_grad, other_grad, weight, other_input
    )
    out_far = second_exchange(out_leave, out_kept_leave)
    grad_parts, pieces, near_pieces, late_ids = together(grad_parts, pieces, near_pieces, token_ids)
    grad_leave, grad_stay, grad_kept_leave, grad_kept_stay = grad_parts
    grad_leave = tp_exchange(grad_leave, 2)
    far_pieces = [ctx_exchange(pieces[step - 1], step) for step in others]
    out_terms = remaining([out_kept_stay, out_stay, out_far])

    own_ids = lax.dynamic_slice_in_dim(late_ids, chip * block_rows, block_rows, axis=0)
    own_hot = (own_ids[:, None] == jnp.arange(FIRST_ID, FIRST_ID + IDS)[None, :]).astype(bf16)
    own_letters = lax.dynamic_slice(embed_table, (FIRST_ID, core * half), (IDS, half))
    own_tokens = jnp.dot(own_hot, own_letters, preferred_element_type=f32)
    block = sum(term.astype(f32) for term in out_terms).reshape(block_rows, half)
    block = (own_tokens + block).astype(bf16)
    line, steps = [block], [[0]]
    for level in range(levels - 1):
        mask = chips >> level + 1
        held = line[0] if level == 0 else jnp.concatenate(line, axis=0)
        came = tp_exchange(held, 2 * mask)
        line.append(came)
        steps.append([step ^ mask for group in steps for step in group])
    outgoing = (grad_kept_leave + grad_leave.astype(f32)).astype(bf16)
    outgoing, grad_stay = together(outgoing, grad_stay)
    grad_far, grad_stay = tp_exchange(outgoing, 4), tp_exchange(grad_stay, 2)
    grad_terms = remaining([grad_kept_stay, grad_stay, grad_far])
    from_neighbour = [tp_exchange(value, 2) for value in line]
    neighbour_steps = [[step ^ 1 for step in group] for group in steps]

    came = from_neighbour[-1]
    line, early_steps = line + from_neighbour[:-1], steps + neighbour_steps[:-1]
    base = run_assemble(chips, early_steps, chip_tie, core_tie, line, [tp_exchange(value, 1) for value in line])
    mine = near_pieces + far_pieces
    output_weight_grad = run_weight_grad(
        me_tie, core_tie, output_grad, hidden, mine, [tp_exchange(value, 1) for value in mine]
    )
    kept_sum = sum(term.astype(f32) for term in grad_terms[:-1])
    base, output_weight_grad, came, kept_sum, last = together(
        base, output_weight_grad, came, kept_sum, grad_terms[-1]
    )
    total = (kept_sum + last.astype(f32)).reshape(2, block_rows // 2, half)
    my_rows, their_rows = pick(total, core), pick(total, 1 - core)
    other_columns = tp_exchange(their_rows, 1)
    block_output = run_insert(neighbour_steps[-1], chip_tie, core_tie, came, tp_exchange(came, 1), base)
    normed_grad = jnp.where(
        core == 0,
        jnp.concatenate([my_rows, other_columns], axis=1),
        jnp.concatenate([other_columns, my_rows], axis=1),
    )
    return (block_output, output_weight_grad, jnp.transpose(projection_grad, (1, 0, 2)), normed_grad)


def solution(mesh):
    in_specs = (
        P("ctx"),
        P(),
        P(),
        P(None, None, "tp"),
        P(None, None, "tp"),
        P("tp", "ctx"),
        P("tp"),
        P(None, "tp"),
        P("ctx", None),
    )
    out_specs = (P("ctx", None), P("ctx", "tp"), P("ctx", None, "tp"), P(("ctx", "tp"), None))
    return jax.shard_map(body, mesh=mesh, in_specs=in_specs, out_specs=out_specs, check_vma=False)
```
